256 devices in a mesh: grp: 8 (over z), seq: 32 (over y, x, core).
Axes of the slice: x: 4, y: 4, z: 8, core: 2. Of those that a mesh axis runs over, the one named last changes fastest.
Arguments:
- queries: bfloat16 [32768, 1024], P(('grp', 'seq')), may hold values from -6 to 6
- key_rows: bfloat16 [32768, 1024], P(('grp', 'seq')), may hold values from -6 to 6
- value_rows: bfloat16 [32768, 1024], P(('grp', 'seq')), may hold values from -6 to 6
- channel_gain: float32 [1024], replicated, may hold values from 0.5 to 1.5
- out_cotangent: bfloat16 [32768, 1024], P(('grp', 'seq')), may hold values from -6 to 6
Outputs:
- attended: bfloat16 [32768, 1024], P(('grp', 'seq'))
- grad_queries: bfloat16 [32768, 1024], P(('grp', 'seq'))
- grad_keys: bfloat16 [32768, 1024], P(('grp', 'seq'))
- grad_values: bfloat16 [32768, 1024], P(('grp', 'seq'))
The draws below stay inside these ranges and needn't reach their ends.
All inputs are finite; a program needn't handle non-finite values.
Results may differ from the reference program's by a relative error of at most 0.0075.
Values sent between devices are 32-bit elements; how exact they have to be, the bound alone decides.
No kernel may reach another device: no remote copies, remote signals or barrier semaphores. Data moves between devices by JAX's collectives and lax.ppermute only.
A program may use at most 256 MiB of HBM per device.

```python
import jax
import jax.numpy as jnp
from jax import lax

HEADS = 8
HEAD_DIM = 128
D = 1024
TOK_DEV = 128
TOKENS = 32768
N_GRP = 8
N_SEQ = 32


def levels(rng, dims, shards, smallest, top_value):
    factor_of = 1.0
    for dim, blocks in shards:
        heights = jax.random.uniform(jax.random.fold_in(jax.random.fold_in(rng, 6), dim), (blocks,), jnp.float32, smallest / len(shards), top_value / len(shards))
        factor_of = factor_of * jnp.repeat(jnp.exp(heights), dims[dim] // blocks).reshape((-1,) + (1,) * (len(dims) - 1 - dim))
    return factor_of


def noise(stream_key, shape, scale, most, pieces=(), kind=jnp.bfloat16):
    gain = levels(stream_key, shape, pieces, -0.22, 0.18) if pieces else 1.0
    values = jax.random.normal(stream_key, shape, jnp.float32) * scale * gain
    return jnp.minimum(jnp.maximum(values, -most), most).astype(kind)


def setup_inputs(seed: int = 0) -> dict:
    key_of = jax.random.split(jax.random.key(seed), 6)
    return {
        "queries": noise(key_of[0], (TOKENS, D), 1.0, 6.0, ((0, 256),)),
        "key_rows": noise(key_of[1], (TOKENS, D), 1.0, 6.0, ((0, 256),)),
        "value_rows": noise(key_of[2], (TOKENS, D), 1.0, 6.0, ((0, 256),)),
        "channel_gain": jnp.clip(1.0 + 0.1 * jax.random.normal(key_of[3], (D,), jnp.float32), 0.5, 1.5),
        "out_cotangent": noise(key_of[4], (TOKENS, D), 1.0, 6.0, ((0, 256),)),
    }


epsilon = 1e-06

def rounded(value):
    return lax.optimization_barrier(value.astype(jnp.bfloat16)).astype(jnp.float32)

def forward_part(query_heads, key_heads, value_heads, earlier):
    length = query_heads.shape[0]
    causal = jnp.arange(length)[:, None] >= jnp.arange(length)[None, :]
    scores = jnp.einsum('the,she->hts', query_heads, key_heads)
    weights = rounded(jnp.where(causal[None], scores, 0.0))
    output = jnp.einsum('hts,shf->thf', weights, value_heads) + jnp.einsum('the,hef->thf', query_heads, rounded(earlier))
    inverse = lax.rsqrt(lax.optimization_barrier(jnp.mean(output * output, axis=-1, keepdims=True)) + epsilon)
    return (output * inverse, inverse, weights, causal)

def delta_part(normed, inverse, grad_heads, gain_heads):
    scaled = grad_heads * gain_heads
    return rounded(inverse * (scaled - normed * lax.optimization_barrier(jnp.mean(scaled * normed, axis=-1, keepdims=True))))

def reference(queries, key_rows, value_rows, channel_gain, out_cotangent):
    blocks = N_GRP * N_SEQ

    def heads(array):
        return array.astype(jnp.float32).reshape(blocks, TOK_DEV, HEADS, HEAD_DIM)
    query_all, key_all, value_all, grad_all = (heads(queries), heads(key_rows), heads(value_rows), heads(out_cotangent))
    gain_heads = channel_gain.astype(jnp.float32).reshape(HEADS, HEAD_DIM)
    states = jnp.einsum('nshe,nshf->nhef', key_all, value_all)
    zero_state = jnp.zeros((1, HEADS, HEAD_DIM, HEAD_DIM), jnp.float32)
    befores = jnp.concatenate([zero_state, jnp.cumsum(states, axis=0)[:-1]], axis=0)

    def first(items):
        query_heads, key_heads, value_heads, grad_heads, earlier = items
        normed, inverse, weights, causal = forward_part(query_heads, key_heads, value_heads, earlier)
        attended = (normed * gain_heads).astype(jnp.bfloat16)
        out_delta = delta_part(normed, inverse, grad_heads, gain_heads)
        return (attended, jnp.einsum('the,thf->hef', query_heads, out_delta))
    attended, grad_states = lax.map(first, (query_all, key_all, value_all, grad_all, befores))
    reversed_sum = jnp.cumsum(grad_states[::-1], axis=0)[::-1]
    afters = jnp.concatenate([reversed_sum[1:], zero_state], axis=0)

    def second(items):
        query_heads, key_heads, value_heads, grad_heads, earlier, suffix = items
        normed, inverse, weights, causal = forward_part(query_heads, key_heads, value_heads, earlier)
        out_delta = delta_part(normed, inverse, grad_heads, gain_heads)
        delta_scores = rounded(jnp.where(causal[None], jnp.einsum('thf,shf->hts', out_delta, value_heads), 0.0))
        earlier_b = rounded(earlier)
        suffix_b = rounded(suffix)
        grad_query = jnp.einsum('hts,she->the', delta_scores, key_heads) + jnp.einsum('thf,hef->the', out_delta, earlier_b)
        grad_key = jnp.einsum('hts,the->she', delta_scores, query_heads) + jnp.einsum('shf,hef->she', value_heads, suffix_b)
        grad_value = jnp.einsum('hts,thf->shf', weights, out_delta) + jnp.einsum('she,hef->shf', key_heads, suffix_b)
        return (grad_query.astype(jnp.bfloat16), grad_key.astype(jnp.bfloat16), grad_value.astype(jnp.bfloat16))
    grad_query, grad_key, grad_value = lax.map(second, (query_all, key_all, value_all, grad_all, befores, afters))
    total_shape = (TOKENS, D)
    return (attended.reshape(total_shape), grad_query.reshape(total_shape), grad_key.reshape(total_shape), grad_value.reshape(total_shape))
```

```python
import functools

import jax
import jax.numpy as jnp
from jax import lax
from jax.experimental import pallas as pl
from jax.experimental.pallas import tpu as pltpu
from jax.sharding import Mesh, PartitionSpec as P

HEADS = 8
HEAD_DIM = 128
TOK = 128
HALF = HEADS // 2
WIDE = HALF * HEAD_DIM
PAIR = 2 * TOK
ROWS = WIDE
EPSILON = 1e-06
F32, BF16 = jnp.float32, jnp.bfloat16

NT = (((1,), (1,)), ((), ()))
TN = (((0,), (0,)), ((), ()))
NN = (((1,), (0,)), ((), ()))


def dot(a, b, dims):
    return lax.dot_general(a, b, dims, preferred_element_type=F32)


def call(body, outs, cost=None):
    return pl.pallas_call(
        body,
        out_shape=[jax.ShapeDtypeStruct(shape, dtype) for shape, dtype in outs],
        compiler_params=pltpu.CompilerParams(vmem_limit_bytes=32 * 2**20),
    )


def halves():
    core = lax.axis_index("core")
    mine = pl.ds(pl.multiple_of(core * WIDE, WIDE), WIDE)
    other = pl.ds(pl.multiple_of((1 - core) * WIDE, WIDE), WIDE)
    return mine, other


def rows():
    core = lax.axis_index("core")
    mine = pl.ds(pl.multiple_of(core * TOK, TOK), TOK)
    other = pl.ds(pl.multiple_of((1 - core) * TOK, TOK), TOK)
    return mine, other


def head(h):
    return pl.ds(h * HEAD_DIM, HEAD_DIM)


def pack_body(a_ref, b_ref, send_ref):
    _, other = halves()
    send_ref[:, :WIDE] = a_ref[:, other].astype(F32)
    send_ref[:, WIDE:] = b_ref[:, other].astype(F32)


def unpack(a_ref, b_ref, got_ref, a2_ref, b2_ref):
    mine, _ = halves()
    own, far = rows()
    a2_ref[own, :] = a_ref[:, mine]
    b2_ref[own, :] = b_ref[:, mine]
    a2_ref[far, :] = got_ref[:, :WIDE].astype(BF16)
    b2_ref[far, :] = got_ref[:, WIDE:].astype(BF16)


def state_body(k_ref, v_ref, got_ref, k2_ref, v2_ref, state_ref, first_ref):
    unpack(k_ref, v_ref, got_ref, k2_ref, v2_ref)
    for h in range(HALF):
        first = dot(k2_ref[:TOK, head(h)], v2_ref[:TOK, head(h)], TN)
        first_ref[head(h), :] = first
        state_ref[head(h), :] = first + dot(k2_ref[TOK:, head(h)], v2_ref[TOK:, head(h)], TN)


def causal():
    return lax.broadcasted_iota(jnp.int32, (TOK, TOK), 0) >= lax.broadcasted_iota(
        jnp.int32, (TOK, TOK), 1
    )


BLOCKS = [(b, pl.ds(b * TOK, TOK)) for b in range(2)]


def intra_body(q_ref, dy_ref, got_ref, k2_ref, v2_ref, q2_ref, dy2_ref, weights_ref, intra_ref):
    unpack(q_ref, dy_ref, got_ref, q2_ref, dy2_ref)
    mask = causal()
    for h in range(HALF):
        for b, at in BLOCKS:
            scores = dot(q2_ref[at, head(h)], k2_ref[at, head(h)], NT)
            weights = jnp.where(mask, scores, 0.0).astype(BF16)
            weights_ref[h, b] = weights
            intra_ref[at, head(h)] = dot(weights, v2_ref[at, head(h)], NN)


def total_body(parts_ref, out_ref):
    total = jnp.sum(parts_ref[...], axis=0)
    for g in range(out_ref.shape[0]):
        out_ref[g] = total


def scan_body(reverse, parts_ref, totals_ref, out_ref):
    place = lax.axis_index("z")
    groups = totals_ref.shape[0]
    running = jnp.zeros(parts_ref.shape[1:], F32)
    for g in range(groups):
        reached = g > place if reverse else g < place
        running = running + jnp.where(reached, totals_ref[g], 0.0)
    steps = parts_ref.shape[0]
    for i in range(steps):
        at = steps - 1 - i if reverse else i
        out_ref[at] = running
        running = running + parts_ref[at]


def entering(before_ref, first_ref, h, b):
    before = before_ref[head(h), :]
    return (before + first_ref[head(h), :] if b else before).astype(BF16)


def mid_body(
    q2_ref, dy2_ref, intra_ref, before_ref, first_ref, gain_ref,
    attended_ref, delta_ref, state_ref, second_ref,
):
    mine, _ = halves()
    gain = gain_ref[:, mine]
    for h in range(HALF):
        gain_h = gain[:, h * HEAD_DIM : (h + 1) * HEAD_DIM]
        states = []
        for b, at in BLOCKS:
            q = q2_ref[at, head(h)]
            out = intra_ref[at, head(h)] + dot(q, entering(before_ref, first_ref, h, b), NN)
            inverse = lax.rsqrt(jnp.mean(out * out, axis=-1, keepdims=True) + EPSILON)
            normed = out * inverse
            attended_ref[at, head(h)] = (normed * gain_h).astype(BF16)
            scaled = dy2_ref[at, head(h)].astype(F32) * gain_h
            mean = jnp.mean(scaled * normed, axis=-1, keepdims=True)
            delta = (inverse * (scaled - normed * mean)).astype(BF16)
            delta_ref[at, head(h)] = delta
            states.append(dot(q, delta, TN))
        second_ref[head(h), :] = states[1]
        state_ref[head(h), :] = states[0] + states[1]


def back_body(
    q2_ref, k2_ref, v2_ref, weights_ref, delta_ref, before_ref, first_ref, attended_ref,
    send_ref, grad_query_ref, grad_key_ref, grad_value_ref, all_ref,
):
    own, far = rows()
    mask = causal()
    for h in range(HALF):
        for b, at in BLOCKS:
            delta = delta_ref[at, head(h)]
            raw = dot(delta, v2_ref[at, head(h)], NT)
            scores = jnp.where(mask, raw, 0.0).astype(BF16)
            all_ref[at, head(h)] = dot(scores, k2_ref[at, head(h)], NN) + dot(
                delta, entering(before_ref, first_ref, h, b), NT
            )
            grad_key_ref[at, head(h)] = dot(scores, q2_ref[at, head(h)], TN)
            grad_value_ref[at, head(h)] = dot(weights_ref[h, b], delta, TN)
    grad_query_ref[...] = all_ref[own, :].astype(BF16)
    send_ref[:, :WIDE] = attended_ref[far, :].astype(F32)
    send_ref[:, WIDE:] = all_ref[far, :].astype(BF16).astype(F32)


def merge_first_body(attended2_ref, mine_ref, got_ref, attended_ref, grad_query_ref):
    mine, other = halves()
    own, _ = rows()
    attended_ref[:, mine] = attended2_ref[own, :]
    attended_ref[:, other] = got_ref[:, :WIDE].astype(BF16)
    grad_query_ref[:, mine] = mine_ref[...]
    grad_query_ref[:, other] = got_ref[:, WIDE:].astype(BF16)


def final_body(k2_ref, v2_ref, after_ref, second_ref, gk_ref, gv_ref, own_ref, send_ref, all_ref):
    own, far = rows()
    for h in range(HALF):
        value = pl.ds(WIDE + h * HEAD_DIM, HEAD_DIM)
        for b, at in BLOCKS:
            after = after_ref[head(h), :]
            after = (after if b else after + second_ref[head(h), :]).astype(BF16)
            all_ref[at, head(h)] = gk_ref[at, head(h)] + dot(v2_ref[at, head(h)], after, NT)
            all_ref[at, value] = gv_ref[at, head(h)] + dot(k2_ref[at, head(h)], after, NN)
    own_ref[...] = all_ref[own, :].astype(BF16)
    send_ref[...] = all_ref[far, :].astype(BF16).astype(F32)


def merge_last_body(own_ref, got_ref, grad_key_ref, grad_value_ref):
    mine, other = halves()
    grad_key_ref[:, mine] = own_ref[:, :WIDE]
    grad_key_ref[:, other] = got_ref[:, :WIDE].astype(BF16)
    grad_value_ref[:, mine] = own_ref[:, WIDE:]
    grad_value_ref[:, other] = got_ref[:, WIDE:].astype(BF16)


def swap(x):
    return lax.ppermute(x, "core", [(0, 1), (1, 0)])


def scan_states(state, reverse):
    plane = lax.axis_size("y") * lax.axis_size("x")
    piece = ROWS // plane
    groups = lax.axis_size("z")
    parts = lax.all_to_all(state.reshape(plane, piece, HEAD_DIM), ("y", "x"), 0, 0, tiled=True)
    (copies,) = call(total_body, [((groups, piece, HEAD_DIM), F32)])(parts)
    totals = lax.all_to_all(copies, "z", 0, 0, tiled=True)
    (scanned,) = call(
        functools.partial(scan_body, reverse), [((plane, piece, HEAD_DIM), F32)]
    )(parts, totals)
    back = lax.all_to_all(scanned, ("y", "x"), 0, 0, tiled=True)
    return back.reshape(ROWS, HEAD_DIM)


def per_device(queries, key_rows, value_rows, channel_gain, out_cotangent):
    own_shape = (TOK, HEADS * HEAD_DIM)
    pair_shape = (PAIR, WIDE)
    (kv_send,) = call(pack_body, [(own_shape, F32)])(key_rows, value_rows)
    kv_got = swap(kv_send)
    (qd_send,) = call(pack_body, [(own_shape, F32)])(queries, out_cotangent)
    qd_got = swap(qd_send)
    states = ((ROWS, HEAD_DIM), F32)
    k2, v2, state, first = call(
        state_body, [(pair_shape, BF16), (pair_shape, BF16), states, states]
    )(key_rows, value_rows, kv_got)
    q2, dy2, weights, intra = call(
        intra_body,
        [(pair_shape, BF16), (pair_shape, BF16), ((HALF, 2, TOK, TOK), BF16), (pair_shape, F32)],
    )(queries, out_cotangent, qd_got, k2, v2)
    before = scan_states(state, False)
    attended2, delta, grad_state, second = call(
        mid_body, [(pair_shape, BF16), (pair_shape, BF16), states, states]
    )(q2, dy2, intra, before, first, channel_gain.reshape(1, -1))
    send, own_query, gk_part, gv_part, _ = call(
        back_body,
        [(own_shape, F32), ((TOK, WIDE), BF16), (pair_shape, F32), (pair_shape, F32), (pair_shape, F32)],
    )(q2, k2, v2, weights, delta, before, first, attended2)
    got = swap(send)
    attended, grad_query = call(merge_first_body, [(own_shape, BF16), (own_shape, BF16)])(
        attended2, own_query, got
    )
    after = scan_states(grad_state, True)
    own_last, send_last, _ = call(
        final_body, [(own_shape, BF16), (own_shape, F32), ((PAIR, 2 * WIDE), F32)]
    )(k2, v2, after, second, gk_part, gv_part)
    grad_key, grad_value = call(merge_last_body, [(own_shape, BF16), (own_shape, BF16)])(
        own_last, swap(send_last)
    )
    return attended, grad_query, grad_key, grad_value


def solution(mesh):
    fine = Mesh(mesh.devices.reshape(8, 4, 4, 2), ("z", "y", "x", "core"))
    placed = P(("z", "y", "x", "core"), None)
    return jax.shard_map(
        per_device,
        mesh=fine,
        in_specs=(placed, placed, placed, P(), placed),
        out_specs=(placed, placed, placed, placed),
        check_vma=False,
    )
```

```python
import functools

import jax
import jax.numpy as jnp
from jax import lax
from jax.experimental import pallas as pl
from jax.experimental.pallas import tpu as pltpu
from jax.sharding import Mesh, PartitionSpec as P

HEADS = 8
HEAD_DIM = 128
TOK = 128
HALF = HEADS // 2
WIDE = HALF * HEAD_DIM
PAIR = 2 * TOK
SIDE, NZ = 4, 8
RUN = SIDE * PAIR
PIECE = HEAD_DIM // SIDE
EPSILON = 1e-06
F32, BF16 = jnp.float32, jnp.bfloat16

NT = (((1,), (1,)), ((), ()))
TN = (((0,), (0,)), ((), ()))
NN = (((1,), (0,)), ((), ()))


def dot(a, b, dims):
    return lax.dot_general(a, b, dims, preferred_element_type=F32)


def call(body, outs, scratch=(), spots=(), cost=None, kept=None, room=12):
    specs = [pl.BlockSpec(memory_space=spot) for spot in spots]
    return pl.pallas_call(
        body,
        out_shape=[jax.ShapeDtypeStruct(shape, dtype) for shape, dtype in outs],
        scratch_shapes=list(scratch),
        compiler_params=pltpu.CompilerParams(vmem_limit_bytes=room * 2**20),
        cost_estimate=cost and pl.CostEstimate(flops=cost, bytes_accessed=0, transcendentals=0),
        **({"in_specs": specs} if specs else {}),
        **({"out_specs": [pl.BlockSpec(memory_space=m) for m in kept]} if kept else {}),
    )


VM, ANY = pltpu.VMEM, pl.ANY


def halves():
    core = lax.axis_index("core")
    mine = pl.ds(pl.multiple_of(core * WIDE, WIDE), WIDE)
    other = pl.ds(pl.multiple_of((1 - core) * WIDE, WIDE), WIDE)
    return mine, other


def rows():
    core = lax.axis_index("core")
    mine = pl.ds(pl.multiple_of(core * TOK, TOK), TOK)
    other = pl.ds(pl.multiple_of((1 - core) * TOK, TOK), TOK)
    return mine, other


def head(h):
    return pl.ds(h * HEAD_DIM, HEAD_DIM)


def block(b):
    return pl.ds(b * TOK, TOK)


def quarter(i):
    return pl.ds(i * PIECE, PIECE)


def line(shift):
    core = lax.axis_index("core")
    place = lax.axis_index("x") * (1 - core) + lax.axis_index("y") * core
    return lax.rem(place + SIDE + shift, SIDE)


def cross(shift):
    core = lax.axis_index("core")
    place = lax.axis_index("y") * (1 - core) + lax.axis_index("x") * core
    return lax.rem(place + SIDE + shift, SIDE)


def chip(across, along):
    core = lax.axis_index("core")
    return across * (SIDE - core * (SIDE - 1)) + along * (1 + core * (SIDE - 1))


def causal():
    return lax.broadcasted_iota(jnp.int32, (TOK, TOK), 0) >= lax.broadcasted_iota(
        jnp.int32, (TOK, TOK), 1
    )


def pack_body(a_ref, b_ref, send_ref):
    _, other = halves()
    send_ref[:, :WIDE] = a_ref[:, other].astype(F32)
    send_ref[:, WIDE:] = b_ref[:, other].astype(F32)


def unpack(ref, got, out_ref):
    mine, _ = halves()
    at, far = rows()
    out_ref[at, :] = ref[:, mine]
    out_ref[far, :] = got.astype(BF16)


def state_body(k_ref, v_ref, got_ref, _, k2_ref, v2_ref, pieces_ref):
    unpack(k_ref, got_ref[:, :WIDE], k2_ref)
    unpack(v_ref, got_ref[:, WIDE:], v2_ref)
    for h in range(HALF):
        state = dot(k2_ref[:, head(h)], v2_ref[:, head(h)], TN)
        for i in range(SIDE):
            pieces_ref[chip(i, h)] = state[i * PIECE : (i + 1) * PIECE]


def spread_body(q_ref, dy_ref, got_ref, k2_ref, v2_ref, q2_ref, dy2_ref, *send_refs):
    unpack(q_ref, got_ref[:, :WIDE], q2_ref)
    unpack(dy_ref, got_ref[:, WIDE:], dy2_ref)
    for s, send_ref in enumerate(send_refs):
        channels = pl.ds(pl.multiple_of(line(s + 1) * HEAD_DIM, HEAD_DIM), HEAD_DIM)
        for i, ref in enumerate((k2_ref, v2_ref, q2_ref, dy2_ref)):
            send_ref[:, head(i)] = ref[:, channels].astype(F32)


def line_body(
    k2_ref, v2_ref, q2_ref, dy2_ref, gain_ref, got1_ref, got2_ref, got3_ref,
    q_ref, dy_ref, gain_out, intra_ref, first_ref, k_ref, v_ref,
):
    refs = (k_ref, v_ref, q_ref, dy_ref)
    place = line(0)
    channels = pl.ds(pl.multiple_of(place * HEAD_DIM, HEAD_DIM), HEAD_DIM)
    at = pl.ds(pl.multiple_of(place * PAIR, PAIR), PAIR)
    for ref, own_ref in zip(refs, (k2_ref, v2_ref, q2_ref, dy2_ref)):
        ref[at, :] = own_ref[:, channels]
    for s, got_ref in enumerate((got1_ref, got2_ref, got3_ref)):
        at = pl.ds(pl.multiple_of(line(-1 - s) * PAIR, PAIR), PAIR)
        for i, ref in enumerate(refs):
            ref[at, :] = got_ref[:, head(i)].astype(BF16)
    whole = lax.axis_index("core") * WIDE + place * HEAD_DIM
    gain = gain_ref[:, pl.ds(pl.multiple_of(whole, HEAD_DIM), HEAD_DIM)]
    gain_out[...] = jnp.broadcast_to(gain, gain_out.shape)
    mask = causal()
    for b in range(2 * SIDE):
        k, v = k_ref[block(b), :], v_ref[block(b), :]
        weights = jnp.where(mask, dot(q_ref[block(b), :], k, NT), 0.0).astype(BF16)
        intra_ref[block(b), :] = dot(weights, v, NN)
        if b % 2 == 0:
            first_ref[b // 2] = dot(k, v, TN)


def plane_body(parts_ref, _, total_ref, sums_ref):
    running = jnp.zeros(parts_ref.shape[1:], F32)
    for p in range(SIDE * SIDE):
        sums_ref[p] = running
        running = running + parts_ref[p]
    for g in range(NZ):
        total_ref[g] = running


def before_body(sums_ref, got_ref, *out_refs):
    z = lax.axis_index("z")
    base = jnp.zeros(got_ref.shape[1:], F32)
    for g in range(NZ - 1):
        base = base + jnp.where(g < z, got_ref[g], 0.0)
    for s, ref in enumerate(out_refs):
        for j in range(SIDE):
            ref[j] = sums_ref[chip(cross(s), j)] + base


def deltas(out, g):
    inverse = lax.rsqrt(jnp.mean(out * out, axis=-1, keepdims=True) + EPSILON)
    normed = out * inverse
    mean = jnp.mean(g * normed, axis=-1, keepdims=True)
    return normed, (inverse * (g - normed * mean)).astype(BF16)


def turn_body(
    q_ref, dy_ref, gain_ref, intra_ref, first_ref, w0, w1, w2, w3,
    p0, p1, p2, p3, before_ref, pairs_ref,
):
    for s, ref in enumerate((w0, w1, w2, w3)):
        at = pl.ds(pl.multiple_of(cross(-s) * PIECE, PIECE), PIECE)
        for j in range(SIDE):
            before_ref[j, at, :] = ref[j]
    gain = gain_ref[:1, :]
    for j in range(SIDE):
        before = before_ref[j]
        for b in range(2):
            at = block(2 * j + b)
            q = q_ref[at, :]
            if b:
                before = before + first_ref[j]
            out = intra_ref[at, :] + dot(q, before.astype(BF16), NN)
            _, delta = deltas(out, dy_ref[at, :].astype(F32) * gain)
            state = dot(q, delta, TN)
            pair = pair + state if b else state
        pairs_ref[j] = pair
    for s, ref in enumerate((p0, p1, p2, p3)):
        at = pl.ds(pl.multiple_of(cross(s) * PIECE, PIECE), PIECE)
        for j in range(SIDE):
            ref[j] = pairs_ref[j, at, :]


def gather_body(p0, p1, p2, p3, before_ref, total_ref, pairs_ref, b0, b1, b2, b3):
    total = jnp.zeros(p0.shape[1:], F32)
    for s, ref in enumerate((p0, p1, p2, p3)):
        for j in range(SIDE):
            pairs_ref[chip(cross(-s), j)] = ref[j]
            total = total + ref[j]
    for g in range(NZ):
        total_ref[g] = total
    for s, ref in enumerate((b0, b1, b2, b3)):
        ref[...] = before_ref[line(s)]


def later_body(pairs_ref, got_ref, _0, _1, _2, out_ref):
    z = lax.axis_index("z")
    running = jnp.zeros(got_ref.shape[1:], F32)
    for g in range(1, NZ):
        running = running + jnp.where(g > z, got_ref[g], 0.0)
    for p in reversed(range(SIDE * SIDE)):
        out_ref[p] = running
        running = running + pairs_ref[p]


def back_body(
    q2_ref, k2_ref, v2_ref, dy2_ref, gain_ref, b0, b1, b2, b3,
    send_ref, own_ref, gk_ref, gv_ref, second_ref, before_ref, all_ref,
):
    mine, _ = halves()
    own, far = rows()
    for s, ref in enumerate((b0, b1, b2, b3)):
        before_ref[line(-s)] = ref[...]
    mask = causal()
    gains = gain_ref[:, mine]
    for h in range(HALF):
        gain = gains[:, h * HEAD_DIM : (h + 1) * HEAD_DIM]
        query = pl.ds(WIDE + h * HEAD_DIM, HEAD_DIM)
        before = before_ref[h]
        for b in range(2):
            at = block(b)
            q, k, v = q2_ref[at, head(h)], k2_ref[at, head(h)], v2_ref[at, head(h)]
            before_b = before.astype(BF16)
            if b == 0:
                before = before + dot(k, v, TN)
            weights = jnp.where(mask, dot(q, k, NT), 0.0).astype(BF16)
            out = dot(weights, v, NN) + dot(q, before_b, NN)
            normed, delta = deltas(out, dy2_ref[at, head(h)].astype(F32) * gain)
            all_ref[at, head(h)] = normed * gain
            scores = jnp.where(mask, dot(delta, v, NT), 0.0).astype(BF16)
            all_ref[at, query] = dot(scores, k, NN) + dot(delta, before_b, NT)
            gk_ref[at, head(h)] = dot(scores, q, TN)
            gv_ref[at, head(h)] = dot(weights, delta, TN)
        second_ref[h] = dot(q, delta, TN)
    own_ref[...] = all_ref[own, :].astype(BF16)
    send_ref[...] = all_ref[far, :].astype(BF16).astype(F32)


def final_body(mine, k2_ref, v2_ref, later_ref, second_ref, gk_ref, gv_ref, out_ref):
    own, far = rows()
    at = own if mine else far
    core = lax.axis_index("core")
    b = core if mine else 1 - core
    for h in range(HALF):
        value = pl.ds(WIDE + h * HEAD_DIM, HEAD_DIM)
        later = jnp.concatenate([later_ref[chip(i, h)] for i in range(SIDE)], axis=0)
        after = (later + jnp.where(b == 0, second_ref[h], 0.0)).astype(BF16)
        gk = gk_ref[at, head(h)] + dot(v2_ref[at, head(h)], after, NT)
        gv = gv_ref[at, head(h)] + dot(k2_ref[at, head(h)], after, NN)
        out_ref[:, head(h)] = gk.astype(BF16).astype(out_ref.dtype)
        out_ref[:, value] = gv.astype(BF16).astype(out_ref.dtype)


def merge_body(own_ref, got_ref, a_ref, b_ref):
    mine, other = halves()
    a_ref[:, mine] = own_ref[:, :WIDE]
    a_ref[:, other] = got_ref[:, :WIDE].astype(BF16)
    b_ref[:, mine] = own_ref[:, WIDE:]
    b_ref[:, other] = got_ref[:, WIDE:].astype(BF16)


def swap(x):
    return lax.ppermute(x, "core", [(0, 1), (1, 0)])


AXES = ("z", "y", "x", "core")


def device(z, core, across, along):
    y, x = (along, across) if core else (across, along)
    return ((z * SIDE + y) * SIDE + x) * 2 + core


def places():
    return [
        (z, core, i, j) for z in range(NZ) for core in range(2) for i in range(SIDE) for j in range(SIDE)
    ]


def shift_line(arrays):
    return [
        lax.ppermute(
            a, AXES, [(device(z, c, i, j), device(z, c, i, (j + s) % SIDE)) for z, c, i, j in places()]
        )
        for s, a in enumerate(arrays, 1)
    ]


def shift_cross(arrays):
    return [
        lax.ppermute(
            a, AXES, [(device(z, c, i, j), device(z, c, (i + s) % SIDE, j)) for z, c, i, j in places()]
        )
        for s, a in enumerate(arrays, 1)
    ]


def per_device(queries, key_rows, value_rows, channel_gain, out_cotangent):
    own_shape = (TOK, HEADS * HEAD_DIM)
    pair = (PAIR, WIDE)
    slices = ((SIDE * SIDE, PIECE, HEAD_DIM), F32)
    copies = ((NZ, PIECE, HEAD_DIM), F32)
    some = ((SIDE, PIECE, HEAD_DIM), F32)
    states = ((SIDE, HEAD_DIM, HEAD_DIM), F32)
    square = ((HEAD_DIM, HEAD_DIM), F32)
    gain = channel_gain.reshape(1, -1)
    pack = call(pack_body, [(own_shape, F32)])
    kv_got = swap(pack(key_rows, value_rows)[0])
    qd_got = swap(pack(queries, out_cotangent)[0])
    k2, v2, pieces = call(state_body, [(pair, BF16), (pair, BF16), slices], spots=(VM,) * 3 + (ANY,))(
        key_rows, value_rows, kv_got, qd_got
    )
    parts = lax.all_to_all(pieces, ("y", "x"), 0, 0, tiled=True)
    q2, dy2, *sends = call(spread_body, [(pair, BF16)] * 2 + [(pair, F32)] * (SIDE - 1))(
        queries, out_cotangent, qd_got, k2, v2
    )
    run = (RUN, HEAD_DIM)
    qh, dyh, gain_h, intra_h, first = call(
        line_body,
        [(run, BF16), (run, BF16), ((8, HEAD_DIM), F32), (run, F32), states],
        [pltpu.VMEM(run, BF16), pltpu.VMEM(run, BF16)],
        cost=10**11,
    )(k2, v2, q2, dy2, gain, *shift_line(sends))
    total, sums = call(plane_body, [copies, slices], spots=(VM, ANY), cost=10**11)(parts, dy2)
    earlier = lax.all_to_all(total, "z", 0, 0, tiled=True)
    w_own, *w_sends = call(before_body, [some] * SIDE)(sums, earlier)
    p_own, p1, p2, p3, before = call(
        turn_body, [some] * SIDE + [states], [pltpu.VMEM(*states)]
    )(qh, dyh, gain_h, intra_h, first, w_own, *shift_cross(w_sends))
    total, pairs, b_own, *b_sends = call(gather_body, [copies, slices] + [square] * SIDE)(
        p_own, *shift_cross((p1, p2, p3)), before
    )
    totals = lax.all_to_all(total, "z", 0, 0, tiled=True)
    b_got = shift_line(b_sends)
    (later,) = call(later_body, [slices], spots=(VM,) * 2 + (ANY,) * 3)(pairs, totals, *b_got)
    send, own, gk, gv, second = call(
        back_body,
        [(own_shape, F32), (own_shape, BF16), (pair, F32), (pair, F32), states],
        [pltpu.VMEM(*states), pltpu.VMEM((PAIR, 2 * WIDE), F32)],
    )(q2, k2, v2, dy2, gain, b_own, *b_got)
    merge = call(merge_body, [(own_shape, BF16), (own_shape, BF16)])
    attended, grad_query = merge(own, swap(send))
    after = lax.all_to_all(later, ("y", "x"), 0, 0, tiled=True)
    last = (k2, v2, after, second, gk, gv)
    (last_send,) = call(functools.partial(final_body, False), [(own_shape, F32)])(*last)
    last_got = swap(last_send)
    (last_own,) = call(functools.partial(final_body, True), [(own_shape, BF16)])(*last)
    grad_key, grad_value = merge(last_own, last_got)
    return attended, grad_query, grad_key, grad_value


def solution(mesh):
    fine = Mesh(mesh.devices.reshape(NZ, SIDE, SIDE, 2), AXES)
    placed = P(AXES, None)
    return jax.shard_map(
        per_device,
        mesh=fine,
        in_specs=(placed, placed, placed, P(), placed),
        out_specs=(placed, placed, placed, placed),
        check_vma=False,
    )
```

```python
import functools

import jax
import jax.numpy as jnp
from jax import lax
from jax.experimental import pallas as pl
from jax.experimental.pallas import tpu as pltpu
from jax.sharding import Mesh, PartitionSpec as P

HEADS = 8
HEAD_DIM = 128
TOK = 128
HALF = HEADS // 2
WIDE = HALF * HEAD_DIM
PAIR = 2 * TOK
SIDE, NZ = 4, 8
RUN = SIDE * PAIR
PIECE = HEAD_DIM // SIDE
EPSILON = 1e-06
F32, BF16 = jnp.float32, jnp.bfloat16

NT = (((1,), (1,)), ((), ()))
TN = (((0,), (0,)), ((), ()))
NN = (((1,), (0,)), ((), ()))


def dot(a, b, dims):
    return lax.dot_general(a, b, dims, preferred_element_type=F32)


def call(body, outs, scratch=(), spots=(), cost=None, kept=None, room=12):
    specs = [pl.BlockSpec(memory_space=spot) for spot in spots]
    return pl.pallas_call(
        body,
        out_shape=[jax.ShapeDtypeStruct(shape, dtype) for shape, dtype in outs],
        scratch_shapes=list(scratch),
        compiler_params=pltpu.CompilerParams(vmem_limit_bytes=room * 2**20),
        cost_estimate=cost and pl.CostEstimate(flops=cost, bytes_accessed=0, transcendentals=0),
        **({"in_specs": specs} if specs else {}),
        **({"out_specs": [pl.BlockSpec(memory_space=m) for m in kept]} if kept else {}),
    )


VM, HBM = pltpu.VMEM, pltpu.HBM
MARK = ((8, HEAD_DIM), jnp.float32)


def mark(ref):
    ref[...] = jnp.zeros_like(ref)


def halves():
    core = lax.axis_index("core")
    mine = pl.ds(pl.multiple_of(core * WIDE, WIDE), WIDE)
    other = pl.ds(pl.multiple_of((1 - core) * WIDE, WIDE), WIDE)
    return mine, other


def rows():
    core = lax.axis_index("core")
    mine = pl.ds(pl.multiple_of(core * TOK, TOK), TOK)
    other = pl.ds(pl.multiple_of((1 - core) * TOK, TOK), TOK)
    return mine, other


def head(h):
    return pl.ds(h * HEAD_DIM, HEAD_DIM)


def block(b):
    return pl.ds(b * TOK, TOK)


def quarter(i):
    return pl.ds(i * PIECE, PIECE)


def line(shift):
    core = lax.axis_index("core")
    place = lax.axis_index("x") * (1 - core) + lax.axis_index("y") * core
    return lax.rem(place + SIDE + shift, SIDE)


def cross(shift):
    core = lax.axis_index("core")
    place = lax.axis_index("y") * (1 - core) + lax.axis_index("x") * core
    return lax.rem(place + SIDE + shift, SIDE)


def chip(across, along):
    core = lax.axis_index("core")
    return across * (SIDE - core * (SIDE - 1)) + along * (1 + core * (SIDE - 1))


def causal():
    return lax.broadcasted_iota(jnp.int32, (TOK, TOK), 0) >= lax.broadcasted_iota(
        jnp.int32, (TOK, TOK), 1
    )


def pack_body(a_ref, b_ref, send_ref, *mark_refs):
    _, other = halves()
    for ref in mark_refs:
        mark(ref)
    send_ref[:, :WIDE] = a_ref[:, other].astype(F32)
    send_ref[:, WIDE:] = b_ref[:, other].astype(F32)


def unpack(ref, got, out_ref):
    mine, _ = halves()
    at, far = rows()
    out_ref[at, :] = ref[:, mine]
    out_ref[far, :] = got.astype(BF16)


def state_body(k_ref, v_ref, got_ref, _, k2_ref, v2_ref, pieces_ref):
    unpack(k_ref, got_ref[:, :WIDE], k2_ref)
    unpack(v_ref, got_ref[:, WIDE:], v2_ref)
    for h in range(HALF):
        state = dot(k2_ref[:, head(h)], v2_ref[:, head(h)], TN)
        for i in range(SIDE):
            pieces_ref[chip(i, h)] = state[i * PIECE : (i + 1) * PIECE]


def spread_body(
    q_ref, dy_ref, got_ref, k2_ref, v2_ref,
    q2_ref, dy2_ref, mark_ref, s1, s2, s3, held_ref, sems,
):
    mark(mark_ref)
    unpack(q_ref, got_ref[:, :WIDE], q2_ref)
    unpack(dy_ref, got_ref[:, WIDE:], dy2_ref)
    copies = []
    for s, send_ref in enumerate((s1, s2, s3)):
        channels = pl.ds(pl.multiple_of(line(s + 1) * HEAD_DIM, HEAD_DIM), HEAD_DIM)
        for i, ref in enumerate((k2_ref, v2_ref, q2_ref, dy2_ref)):
            held_ref[s, :, head(i)] = ref[:, channels].astype(F32)
        copies.append(pltpu.make_async_copy(held_ref.at[s], send_ref, sems.at[s]))
        copies[-1].start()
    for copy in copies:
        copy.wait()


def line_body(
    k2_ref, v2_ref, q2_ref, dy2_ref, gain_ref, got1_ref, got2_ref, got3_ref,
    q_ref, dy_ref, gain_out, intra_ref, first_ref, k_ref, v_ref,
):
    refs = (k_ref, v_ref, q_ref, dy_ref)
    place = line(0)
    channels = pl.ds(pl.multiple_of(place * HEAD_DIM, HEAD_DIM), HEAD_DIM)
    at = pl.ds(pl.multiple_of(place * PAIR, PAIR), PAIR)
    for ref, own_ref in zip(refs, (k2_ref, v2_ref, q2_ref, dy2_ref)):
        ref[at, :] = own_ref[:, channels]
    for s, got_ref in enumerate((got1_ref, got2_ref, got3_ref)):
        at = pl.ds(pl.multiple_of(line(-1 - s) * PAIR, PAIR), PAIR)
        for i, ref in enumerate(refs):
            ref[at, :] = got_ref[:, head(i)].astype(BF16)
    whole = lax.axis_index("core") * WIDE + place * HEAD_DIM
    gain = gain_ref[:, pl.ds(pl.multiple_of(whole, HEAD_DIM), HEAD_DIM)]
    gain_out[...] = jnp.broadcast_to(gain, gain_out.shape)
    mask = causal()
    for b in range(2 * SIDE):
        k, v = k_ref[block(b), :], v_ref[block(b), :]
        weights = jnp.where(mask, dot(q_ref[block(b), :], k, NT), 0.0).astype(BF16)
        intra_ref[block(b), :] = dot(weights, v, NN)
        if b % 2 == 0:
            first_ref[b // 2] = dot(k, v, TN)


def plane_body(parts_ref, _, total_ref, sums_ref):
    running = jnp.zeros(parts_ref.shape[1:], F32)
    for p in range(SIDE * SIDE):
        sums_ref[p] = running
        running = running + parts_ref[p]
    for g in range(NZ):
        total_ref[g] = running


def before_body(sums_ref, got_ref, *out_refs):
    z = lax.axis_index("z")
    base = jnp.zeros(got_ref.shape[1:], F32)
    for g in range(NZ - 1):
        base = base + jnp.where(g < z, got_ref[g], 0.0)
    for s, ref in enumerate(out_refs):
        for j in range(SIDE):
            ref[j] = sums_ref[chip(cross(s), j)] + base


def deltas(out, g):
    inverse = lax.rsqrt(jnp.mean(out * out, axis=-1, keepdims=True) + EPSILON)
    normed = out * inverse
    mean = jnp.mean(g * normed, axis=-1, keepdims=True)
    return normed, (inverse * (g - normed * mean)).astype(BF16)


def turn_body(
    q_ref, dy_ref, gain_ref, intra_ref, first_ref, w0, w1, w2, w3,
    p0, p1, p2, p3, b0, b1, b2, b3, before_ref, pairs_ref,
):
    for s, ref in enumerate((w0, w1, w2, w3)):
        at = pl.ds(pl.multiple_of(cross(-s) * PIECE, PIECE), PIECE)
        for j in range(SIDE):
            before_ref[j, at, :] = ref[j]
    gain = gain_ref[:1, :]
    for j in range(SIDE):
        before = before_ref[j]
        for b in range(2):
            at = block(2 * j + b)
            q = q_ref[at, :]
            if b:
                before = before + first_ref[j]
            out = intra_ref[at, :] + dot(q, before.astype(BF16), NN)
            _, delta = deltas(out, dy_ref[at, :].astype(F32) * gain)
            state = dot(q, delta, TN)
            pair = pair + state if b else state
        pairs_ref[j] = pair
    for s, ref in enumerate((p0, p1, p2, p3)):
        at = pl.ds(pl.multiple_of(cross(s) * PIECE, PIECE), PIECE)
        for j in range(SIDE):
            ref[j] = pairs_ref[j, at, :]
    for s, ref in enumerate((b0, b1, b2, b3)):
        ref[...] = before_ref[line(s)]


def gather_body(p0, p1, p2, p3, total_ref, pairs_ref):
    total = jnp.zeros(p0.shape[1:], F32)
    for s, ref in enumerate((p0, p1, p2, p3)):
        for j in range(SIDE):
            pairs_ref[chip(cross(-s), j)] = ref[j]
            total = total + ref[j]
    for g in range(NZ):
        total_ref[g] = total


def later_body(pairs_ref, got_ref, _, out_ref):
    z = lax.axis_index("z")
    running = jnp.zeros(got_ref.shape[1:], F32)
    for g in range(1, NZ):
        running = running + jnp.where(g > z, got_ref[g], 0.0)
    for p in reversed(range(SIDE * SIDE)):
        out_ref[p] = running
        running = running + pairs_ref[p]


def query_body(
    q2_ref, k2_ref, v2_ref, dy2_ref, gain_ref, b0, b1, b2, b3,
    mark_ref, send_ref, own_ref, delta_ref, before_ref, all_ref,
):
    mark(mark_ref)
    mine, _ = halves()
    own, far = rows()
    for s, ref in enumerate((b0, b1, b2, b3)):
        before_ref[line(-s)] = ref[...]
    mask = causal()
    gains = gain_ref[:, mine]
    for h in range(HALF):
        gain = gains[:, h * HEAD_DIM : (h + 1) * HEAD_DIM]
        query = pl.ds(WIDE + h * HEAD_DIM, HEAD_DIM)
        before = before_ref[h]
        for b in range(2):
            at = block(b)
            q, k, v = q2_ref[at, head(h)], k2_ref[at, head(h)], v2_ref[at, head(h)]
            before_b = before.astype(BF16)
            if b == 0:
                before = before + dot(k, v, TN)
            weights = jnp.where(mask, dot(q, k, NT), 0.0).astype(BF16)
            out = dot(weights, v, NN) + dot(q, before_b, NN)
            normed, delta = deltas(out, dy2_ref[at, head(h)].astype(F32) * gain)
            delta_ref[at, head(h)] = delta
            all_ref[at, head(h)] = normed * gain
            scores = jnp.where(mask, dot(delta, v, NT), 0.0).astype(BF16)
            all_ref[at, query] = dot(scores, k, NN) + dot(delta, before_b, NT)
    own_ref[...] = all_ref[own, :].astype(BF16)
    send_ref[...] = all_ref[far, :].astype(BF16).astype(F32)


def keys_body(q2_ref, k2_ref, v2_ref, delta_ref, gk_ref, gv_ref, second_ref):
    mask = causal()
    for h in range(HALF):
        for b in range(2):
            at = block(b)
            q, k, v = q2_ref[at, head(h)], k2_ref[at, head(h)], v2_ref[at, head(h)]
            delta = delta_ref[at, head(h)]
            weights = jnp.where(mask, dot(q, k, NT), 0.0).astype(BF16)
            scores = jnp.where(mask, dot(delta, v, NT), 0.0).astype(BF16)
            gk_ref[at, head(h)] = dot(scores, q, TN)
            gv_ref[at, head(h)] = dot(weights, delta, TN)
        second_ref[h] = dot(q, delta, TN)


def final_body(mine, k2_ref, v2_ref, later_ref, second_ref, gk_ref, gv_ref, out_ref):
    own, far = rows()
    at = own if mine else far
    core = lax.axis_index("core")
    b = core if mine else 1 - core
    for h in range(HALF):
        value = pl.ds(WIDE + h * HEAD_DIM, HEAD_DIM)
        later = jnp.concatenate([later_ref[chip(i, h)] for i in range(SIDE)], axis=0)
        after = (later + jnp.where(b == 0, second_ref[h], 0.0)).astype(BF16)
        gk = gk_ref[at, head(h)] + dot(v2_ref[at, head(h)], after, NT)
        gv = gv_ref[at, head(h)] + dot(k2_ref[at, head(h)], after, NN)
        out_ref[:, head(h)] = gk.astype(BF16).astype(out_ref.dtype)
        out_ref[:, value] = gv.astype(BF16).astype(out_ref.dtype)


def merge_body(own_ref, got_ref, a_ref, b_ref):
    mine, other = halves()
    a_ref[:, mine] = own_ref[:, :WIDE]
    a_ref[:, other] = got_ref[:, :WIDE].astype(BF16)
    b_ref[:, mine] = own_ref[:, WIDE:]
    b_ref[:, other] = got_ref[:, WIDE:].astype(BF16)


def swap(x):
    return lax.ppermute(x, "core", [(0, 1), (1, 0)])


AXES = ("z", "y", "x", "core")


def device(z, core, across, along):
    y, x = (along, across) if core else (across, along)
    return ((z * SIDE + y) * SIDE + x) * 2 + core


def places():
    return [
        (z, core, i, j) for z in range(NZ) for core in range(2) for i in range(SIDE) for j in range(SIDE)
    ]


def shift_line(arrays):
    return [
        lax.ppermute(
            a, AXES, [(device(z, c, i, j), device(z, c, i, (j + s) % SIDE)) for z, c, i, j in places()]
        )
        for s, a in enumerate(arrays, 1)
    ]


def shift_cross(arrays):
    return [
        lax.ppermute(
            a, AXES, [(device(z, c, i, j), device(z, c, (i + s) % SIDE, j)) for z, c, i, j in places()]
        )
        for s, a in enumerate(arrays, 1)
    ]


def per_device(queries, key_rows, value_rows, channel_gain, out_cotangent):
    own_shape = (TOK, HEADS * HEAD_DIM)
    pair = (PAIR, WIDE)
    slices = ((SIDE * SIDE, PIECE, HEAD_DIM), F32)
    copies = ((NZ, PIECE, HEAD_DIM), F32)
    some = ((SIDE, PIECE, HEAD_DIM), F32)
    states = ((SIDE, HEAD_DIM, HEAD_DIM), F32)
    square = ((HEAD_DIM, HEAD_DIM), F32)
    gain = channel_gain.reshape(1, -1)
    start = (1 - lax.axis_index("core")) * WIDE
    kv_send = jnp.concatenate(
        [lax.dynamic_slice_in_dim(a, start, WIDE, 1) for a in (key_rows, value_rows)], axis=1
    ).astype(F32)
    kv_got = swap(kv_send)
    qd_send, pack_done = call(pack_body, [(own_shape, F32), MARK])(queries, out_cotangent)
    qd_got = swap(qd_send)
    k2, v2, pieces = call(state_body, [(pair, BF16), (pair, BF16), slices], spots=(VM,) * 4)(
        key_rows, value_rows, kv_got, pack_done
    )
    parts = lax.all_to_all(pieces, ("y", "x"), 0, 0, tiled=True)
    q2, dy2, spread_done, *sends = call(
        spread_body,
        [(pair, BF16)] * 2 + [MARK] + [(pair, F32)] * (SIDE - 1),
        [pltpu.VMEM((SIDE - 1,) + pair, F32), pltpu.SemaphoreType.DMA((SIDE - 1,))],
        kept=(VM,) * 3 + (HBM,) * 3,
    )(queries, out_cotangent, qd_got, k2, v2)
    run = (RUN, HEAD_DIM)
    qh, dyh, gain_h, intra_h, first = call(
        line_body,
        [(run, BF16), (run, BF16), ((8, HEAD_DIM), F32), (run, F32), states],
        [pltpu.VMEM(run, BF16), pltpu.VMEM(run, BF16)],
        cost=10**11,
    )(k2, v2, q2, dy2, gain, *shift_line(sends))
    total, sums = call(plane_body, [copies, slices], spots=(VM, VM), cost=10**11)(parts, spread_done)
    earlier = lax.all_to_all(total, "z", 0, 0, tiled=True)
    w_own, *w_sends = call(before_body, [some] * SIDE)(sums, earlier)
    p_own, p1, p2, p3, b_own, *b_sends = call(
        turn_body,
        [some] * SIDE + [square] * SIDE,
        [pltpu.VMEM(*states), pltpu.VMEM(*states)],
    )(qh, dyh, gain_h, intra_h, first, w_own, *shift_cross(w_sends))
    b_got = shift_line(b_sends)
    total, pairs = call(gather_body, [copies, slices])(p_own, *shift_cross((p1, p2, p3)))
    totals = lax.all_to_all(total, "z", 0, 0, tiled=True)
    query_done, send, own, delta = call(
        query_body,
        [MARK, (own_shape, F32), (own_shape, BF16), (pair, BF16)],
        [pltpu.VMEM(*states), pltpu.VMEM((PAIR, 2 * WIDE), F32)],
        cost=10**11,
    )(q2, k2, v2, dy2, gain, b_own, *b_got)
    (later,) = call(later_body, [slices], spots=(VM,) * 3)(pairs, totals, query_done)
    gk, gv, second = call(keys_body, [(pair, F32), (pair, F32), states])(q2, k2, v2, delta)
    merge = call(merge_body, [(own_shape, BF16), (own_shape, BF16)])
    attended, grad_query = merge(own, swap(send))
    after = lax.all_to_all(later, ("y", "x"), 0, 0, tiled=True)
    last = (k2, v2, after, second, gk, gv)
    (last_send,) = call(functools.partial(final_body, False), [(own_shape, F32)])(*last)
    last_got = swap(last_send)
    (last_own,) = call(functools.partial(final_body, True), [(own_shape, BF16)])(*last)
    grad_key, grad_value = merge(last_own, last_got)
    return attended, grad_query, grad_key, grad_value


def solution(mesh):
    fine = Mesh(mesh.devices.reshape(NZ, SIDE, SIDE, 2), AXES)
    placed = P(AXES, None)
    return jax.shard_map(
        per_device,
        mesh=fine,
        in_specs=(placed, placed, placed, P(), placed),
        out_specs=(placed, placed, placed, placed),
        check_vma=False,
    )
```

```python
import functools

import jax
import jax.numpy as jnp
from jax import lax
from jax.experimental import pallas as pl
from jax.experimental.pallas import tpu as pltpu
from jax.sharding import Mesh, PartitionSpec as P

HEADS = 8
HEAD_DIM = 128
TOK = 128
HALF = HEADS // 2
WIDE = HALF * HEAD_DIM
PAIR = 2 * TOK
SIDE, NZ = 4, 8
RUN = SIDE * PAIR
PIECE = HEAD_DIM // SIDE
EPSILON = 1e-06
F32, BF16 = jnp.float32, jnp.bfloat16

NT = (((1,), (1,)), ((), ()))
TN = (((0,), (0,)), ((), ()))
NN = (((1,), (0,)), ((), ()))


def dot(a, b, dims):
    return lax.dot_general(a, b, dims, preferred_element_type=F32)


def call(body, outs, scratch=(), spots=(), cost=None, kept=None, room=12):
    specs = [pl.BlockSpec(memory_space=spot) for spot in spots]
    return pl.pallas_call(
        body,
        out_shape=[jax.ShapeDtypeStruct(shape, dtype) for shape, dtype in outs],
        scratch_shapes=list(scratch),
        compiler_params=pltpu.CompilerParams(vmem_limit_bytes=room * 2**20),
        cost_estimate=cost and pl.CostEstimate(flops=cost, bytes_accessed=0, transcendentals=0),
        **({"in_specs": specs} if specs else {}),
        **({"out_specs": [pl.BlockSpec(memory_space=m) for m in kept]} if kept else {}),
    )


VM, HBM = pltpu.VMEM, pltpu.HBM
MARK = ((8, HEAD_DIM), jnp.float32)


def mark(ref):
    ref[...] = jnp.zeros_like(ref)


def halves():
    core = lax.axis_index("core")
    mine = pl.ds(pl.multiple_of(core * WIDE, WIDE), WIDE)
    other = pl.ds(pl.multiple_of((1 - core) * WIDE, WIDE), WIDE)
    return mine, other


def rows():
    core = lax.axis_index("core")
    mine = pl.ds(pl.multiple_of(core * TOK, TOK), TOK)
    other = pl.ds(pl.multiple_of((1 - core) * TOK, TOK), TOK)
    return mine, other


def head(h):
    return pl.ds(h * HEAD_DIM, HEAD_DIM)


def block(b):
    return pl.ds(b * TOK, TOK)


def quarter(i):
    return pl.ds(i * PIECE, PIECE)


def line(shift):
    core = lax.axis_index("core")
    place = lax.axis_index("x") * (1 - core) + lax.axis_index("y") * core
    return lax.rem(place + SIDE + shift, SIDE)


def cross(shift):
    core = lax.axis_index("core")
    place = lax.axis_index("y") * (1 - core) + lax.axis_index("x") * core
    return lax.rem(place + SIDE + shift, SIDE)


def chip(across, along):
    core = lax.axis_index("core")
    return across * (SIDE - core * (SIDE - 1)) + along * (1 + core * (SIDE - 1))


def causal():
    return lax.broadcasted_iota(jnp.int32, (TOK, TOK), 0) >= lax.broadcasted_iota(
        jnp.int32, (TOK, TOK), 1
    )


def pack_body(a_ref, b_ref, send_ref, *mark_refs):
    _, other = halves()
    for ref in mark_refs:
        mark(ref)
    send_ref[:, :WIDE] = a_ref[:, other].astype(F32)
    send_ref[:, WIDE:] = b_ref[:, other].astype(F32)


def unpack(ref, got, out_ref):
    mine, _ = halves()
    at, far = rows()
    out_ref[at, :] = ref[:, mine]
    out_ref[far, :] = got.astype(BF16)


def state_body(k_ref, v_ref, got_ref, _, k2_ref, v2_ref, pieces_ref):
    unpack(k_ref, got_ref[:, :WIDE], k2_ref)
    unpack(v_ref, got_ref[:, WIDE:], v2_ref)
    for h in range(HALF):
        state = dot(k2_ref[:, head(h)], v2_ref[:, head(h)], TN)
        for i in range(SIDE):
            pieces_ref[chip(i, h)] = state[i * PIECE : (i + 1) * PIECE]


def spread_body(
    q_ref, dy_ref, got_ref, k2_ref, v2_ref,
    q2_ref, dy2_ref, mark_ref, s1, s2, s3, held_ref, sems,
):
    mark(mark_ref)
    unpack(q_ref, got_ref[:, :WIDE], q2_ref)
    unpack(dy_ref, got_ref[:, WIDE:], dy2_ref)
    copies = []
    for s, send_ref in enumerate((s1, s2, s3)):
        channels = pl.ds(pl.multiple_of(line(s + 1) * HEAD_DIM, HEAD_DIM), HEAD_DIM)
        for i, ref in enumerate((k2_ref, v2_ref, q2_ref, dy2_ref)):
            held_ref[s, :, head(i)] = ref[:, channels].astype(F32)
        copies.append(pltpu.make_async_copy(held_ref.at[s], send_ref, sems.at[s]))
        copies[-1].start()
    for copy in copies:
        copy.wait()


def line_body(
    k2_ref, v2_ref, q2_ref, dy2_ref, gain_ref, got1_ref, got2_ref, got3_ref,
    q_ref, dy_ref, gain_out, intra_ref, first_ref, k_ref, v_ref,
):
    refs = (k_ref, v_ref, q_ref, dy_ref)
    place = line(0)
    channels = pl.ds(pl.multiple_of(place * HEAD_DIM, HEAD_DIM), HEAD_DIM)
    at = pl.ds(pl.multiple_of(place * PAIR, PAIR), PAIR)
    for ref, own_ref in zip(refs, (k2_ref, v2_ref, q2_ref, dy2_ref)):
        ref[at, :] = own_ref[:, channels]
    for s, got_ref in enumerate((got1_ref, got2_ref, got3_ref)):
        at = pl.ds(pl.multiple_of(line(-1 - s) * PAIR, PAIR), PAIR)
        for i, ref in enumerate(refs):
            ref[at, :] = got_ref[:, head(i)].astype(BF16)
    whole = lax.axis_index("core") * WIDE + place * HEAD_DIM
    gain = gain_ref[:, pl.ds(pl.multiple_of(whole, HEAD_DIM), HEAD_DIM)]
    gain_out[...] = jnp.broadcast_to(gain, gain_out.shape)
    mask = causal()
    for b in range(2 * SIDE):
        k, v = k_ref[block(b), :], v_ref[block(b), :]
        weights = jnp.where(mask, dot(q_ref[block(b), :], k, NT), 0.0).astype(BF16)
        intra_ref[block(b), :] = dot(weights, v, NN)
        if b % 2 == 0:
            first_ref[b // 2] = dot(k, v, TN)


def plane_body(parts_ref, _, total_ref, sums_ref):
    running = jnp.zeros(parts_ref.shape[1:], F32)
    for p in range(SIDE * SIDE):
        sums_ref[p] = running
        running = running + parts_ref[p]
    for g in range(NZ):
        total_ref[g] = running


def before_body(sums_ref, got_ref, *out_refs):
    z = lax.axis_index("z")
    base = jnp.zeros(got_ref.shape[1:], F32)
    for g in range(NZ - 1):
        base = base + jnp.where(g < z, got_ref[g], 0.0)
    for s, ref in enumerate(out_refs):
        for j in range(SIDE):
            ref[j] = sums_ref[chip(cross(s), j)] + base


def deltas(out, g):
    inverse = lax.rsqrt(jnp.mean(out * out, axis=-1, keepdims=True) + EPSILON)
    normed = out * inverse
    mean = jnp.mean(g * normed, axis=-1, keepdims=True)
    return normed, (inverse * (g - normed * mean)).astype(BF16)


def turn_body(
    q_ref, dy_ref, gain_ref, intra_ref, first_ref, w0, w1, w2, w3,
    p0, p1, p2, p3, before_ref, pairs_ref,
):
    for s, ref in enumerate((w0, w1, w2, w3)):
        at = pl.ds(pl.multiple_of(cross(-s) * PIECE, PIECE), PIECE)
        for j in range(SIDE):
            before_ref[j, at, :] = ref[j]
    gain = gain_ref[:1, :]
    for j in range(SIDE):
        before = before_ref[j]
        for b in range(2):
            at = block(2 * j + b)
            q = q_ref[at, :]
            if b:
                before = before + first_ref[j]
            out = intra_ref[at, :] + dot(q, before.astype(BF16), NN)
            _, delta = deltas(out, dy_ref[at, :].astype(F32) * gain)
            state = dot(q, delta, TN)
            pair = pair + state if b else state
        pairs_ref[j] = pair
    for s, ref in enumerate((p0, p1, p2, p3)):
        at = pl.ds(pl.multiple_of(cross(s) * PIECE, PIECE), PIECE)
        for j in range(SIDE):
            ref[j] = pairs_ref[j, at, :]


def gather_body(p0, p1, p2, p3, before_ref, total_ref, pairs_ref, b0, b1, b2, b3):
    total = jnp.zeros(p0.shape[1:], F32)
    for s, ref in enumerate((p0, p1, p2, p3)):
        for j in range(SIDE):
            pairs_ref[chip(cross(-s), j)] = ref[j]
            total = total + ref[j]
    for g in range(NZ):
        total_ref[g] = total
    for s, ref in enumerate((b0, b1, b2, b3)):
        ref[...] = before_ref[line(s)]


def later_body(pairs_ref, got_ref, out_ref):
    z = lax.axis_index("z")
    running = jnp.zeros(got_ref.shape[1:], F32)
    for g in range(1, NZ):
        running = running + jnp.where(g > z, got_ref[g], 0.0)
    for p in reversed(range(SIDE * SIDE)):
        out_ref[p] = running
        running = running + pairs_ref[p]


def back_body(
    q2_ref, k2_ref, v2_ref, dy2_ref, gain_ref, b0, b1, b2, b3,
    send_ref, own_ref, gk_ref, gv_ref, second_ref, before_ref, all_ref,
):
    mine, _ = halves()
    own, far = rows()
    for s, ref in enumerate((b0, b1, b2, b3)):
        before_ref[line(-s)] = ref[...]
    mask = causal()
    gains = gain_ref[:, mine]
    for h in range(HALF):
        gain = gains[:, h * HEAD_DIM : (h + 1) * HEAD_DIM]
        query = pl.ds(WIDE + h * HEAD_DIM, HEAD_DIM)
        before = before_ref[h]
        for b in range(2):
            at = block(b)
            q, k, v = q2_ref[at, head(h)], k2_ref[at, head(h)], v2_ref[at, head(h)]
            before_b = before.astype(BF16)
            if b == 0:
                before = before + dot(k, v, TN)
            weights = jnp.where(mask, dot(q, k, NT), 0.0).astype(BF16)
            out = dot(weights, v, NN) + dot(q, before_b, NN)
            normed, delta = deltas(out, dy2_ref[at, head(h)].astype(F32) * gain)
            all_ref[at, head(h)] = normed * gain
            scores = jnp.where(mask, dot(delta, v, NT), 0.0).astype(BF16)
            all_ref[at, query] = dot(scores, k, NN) + dot(delta, before_b, NT)
            gk_ref[at, head(h)] = dot(scores, q, TN)
            gv_ref[at, head(h)] = dot(weights, delta, TN)
        second_ref[h] = dot(q, delta, TN)
    own_ref[...] = all_ref[own, :].astype(BF16)
    send_ref[...] = all_ref[far, :].astype(BF16).astype(F32)


def final_body(mine, k2_ref, v2_ref, later_ref, second_ref, gk_ref, gv_ref, out_ref):
    own, far = rows()
    at = own if mine else far
    core = lax.axis_index("core")
    b = core if mine else 1 - core
    for h in range(HALF):
        value = pl.ds(WIDE + h * HEAD_DIM, HEAD_DIM)
        later = jnp.concatenate([later_ref[chip(i, h)] for i in range(SIDE)], axis=0)
        after = (later + jnp.where(b == 0, second_ref[h], 0.0)).astype(BF16)
        gk = gk_ref[at, head(h)] + dot(v2_ref[at, head(h)], after, NT)
        gv = gv_ref[at, head(h)] + dot(k2_ref[at, head(h)], after, NN)
        out_ref[:, head(h)] = gk.astype(BF16).astype(out_ref.dtype)
        out_ref[:, value] = gv.astype(BF16).astype(out_ref.dtype)


def merge_body(own_ref, got_ref, a_ref, b_ref):
    mine, other = halves()
    a_ref[:, mine] = own_ref[:, :WIDE]
    a_ref[:, other] = got_ref[:, :WIDE].astype(BF16)
    b_ref[:, mine] = own_ref[:, WIDE:]
    b_ref[:, other] = got_ref[:, WIDE:].astype(BF16)


def swap(x):
    return lax.ppermute(x, "core", [(0, 1), (1, 0)])


AXES = ("z", "y", "x", "core")


def device(z, core, across, along):
    y, x = (along, across) if core else (across, along)
    return ((z * SIDE + y) * SIDE + x) * 2 + core


def places():
    return [
        (z, core, i, j) for z in range(NZ) for core in range(2) for i in range(SIDE) for j in range(SIDE)
    ]


def shift_line(arrays):
    return [
        lax.ppermute(
            a, AXES, [(device(z, c, i, j), device(z, c, i, (j + s) % SIDE)) for z, c, i, j in places()]
        )
        for s, a in enumerate(arrays, 1)
    ]


def shift_cross(arrays):
    return [
        lax.ppermute(
            a, AXES, [(device(z, c, i, j), device(z, c, (i + s) % SIDE, j)) for z, c, i, j in places()]
        )
        for s, a in enumerate(arrays, 1)
    ]


def per_device(queries, key_rows, value_rows, channel_gain, out_cotangent):
    own_shape = (TOK, HEADS * HEAD_DIM)
    pair = (PAIR, WIDE)
    slices = ((SIDE * SIDE, PIECE, HEAD_DIM), F32)
    copies = ((NZ, PIECE, HEAD_DIM), F32)
    some = ((SIDE, PIECE, HEAD_DIM), F32)
    states = ((SIDE, HEAD_DIM, HEAD_DIM), F32)
    square = ((HEAD_DIM, HEAD_DIM), F32)
    gain = channel_gain.reshape(1, -1)
    start = (1 - lax.axis_index("core")) * WIDE
    kv_send = jnp.concatenate(
        [lax.dynamic_slice_in_dim(a, start, WIDE, 1) for a in (key_rows, value_rows)], axis=1
    ).astype(F32)
    kv_got = swap(kv_send)
    qd_send, pack_done = call(pack_body, [(own_shape, F32), MARK])(queries, out_cotangent)
    qd_got = swap(qd_send)
    k2, v2, pieces = call(state_body, [(pair, BF16), (pair, BF16), slices], spots=(VM,) * 4)(
        key_rows, value_rows, kv_got, pack_done
    )
    parts = lax.all_to_all(pieces, ("y", "x"), 0, 0, tiled=True)
    q2, dy2, spread_done, *sends = call(
        spread_body,
        [(pair, BF16)] * 2 + [MARK] + [(pair, F32)] * (SIDE - 1),
        [pltpu.VMEM((SIDE - 1,) + pair, F32), pltpu.SemaphoreType.DMA((SIDE - 1,))],
        kept=(VM,) * 3 + (HBM,) * 3,
    )(queries, out_cotangent, qd_got, k2, v2)
    run = (RUN, HEAD_DIM)
    qh, dyh, gain_h, intra_h, first = call(
        line_body,
        [(run, BF16), (run, BF16), ((8, HEAD_DIM), F32), (run, F32), states],
        [pltpu.VMEM(run, BF16), pltpu.VMEM(run, BF16)],
        cost=10**11,
    )(k2, v2, q2, dy2, gain, *shift_line(sends))
    total, sums = call(plane_body, [copies, slices], spots=(VM, VM), cost=10**11)(parts, spread_done)
    earlier = lax.all_to_all(total, "z", 0, 0, tiled=True)
    w_own, *w_sends = call(before_body, [some] * SIDE)(sums, earlier)
    p_own, p1, p2, p3, before = call(
        turn_body, [some] * SIDE + [states], [pltpu.VMEM(*states)]
    )(qh, dyh, gain_h, intra_h, first, w_own, *shift_cross(w_sends))
    total, pairs, b_own, *b_sends = call(gather_body, [copies, slices] + [square] * SIDE)(
        p_own, *shift_cross((p1, p2, p3)), before
    )
    totals = lax.all_to_all(total, "z", 0, 0, tiled=True)
    b_got = shift_line(b_sends)
    (later,) = call(later_body, [slices], cost=10**11)(pairs, totals)
    send, own, gk, gv, second = call(
        back_body,
        [(own_shape, F32), (own_shape, BF16), (pair, F32), (pair, F32), states],
        [pltpu.VMEM(*states), pltpu.VMEM((PAIR, 2 * WIDE), F32)],
        cost=10**11,
    )(q2, k2, v2, dy2, gain, b_own, *b_got)
    merge = call(merge_body, [(own_shape, BF16), (own_shape, BF16)])
    attended, grad_query = merge(own, swap(send))
    after = lax.all_to_all(later, ("y", "x"), 0, 0, tiled=True)
    last = (k2, v2, after, second, gk, gv)
    (last_send,) = call(functools.partial(final_body, False), [(own_shape, F32)])(*last)
    last_got = swap(last_send)
    (last_own,) = call(functools.partial(final_body, True), [(own_shape, BF16)])(*last)
    grad_key, grad_value = merge(last_own, last_got)
    return attended, grad_query, grad_key, grad_value


def solution(mesh):
    fine = Mesh(mesh.devices.reshape(NZ, SIDE, SIDE, 2), AXES)
    placed = P(AXES, None)
    return jax.shard_map(
        per_device,
        mesh=fine,
        in_specs=(placed, placed, placed, P(), placed),
        out_specs=(placed, placed, placed, placed),
        check_vma=False,
    )
```

```python
import functools

import jax
import jax.numpy as jnp
from jax import lax
from jax.experimental import pallas as pl
from jax.experimental.pallas import tpu as pltpu
from jax.sharding import Mesh, PartitionSpec as P

HEADS = 8
HEAD_DIM = 128
TOK = 128
HALF = HEADS // 2
WIDE = HALF * HEAD_DIM
PAIR = 2 * TOK
SIDE, NZ = 4, 8
RUN = SIDE * PAIR
PIECE = HEAD_DIM // SIDE
EPSILON = 1e-06
F32, BF16 = jnp.float32, jnp.bfloat16

NT = (((1,), (1,)), ((), ()))
TN = (((0,), (0,)), ((), ()))
NN = (((1,), (0,)), ((), ()))


def dot(a, b, dims):
    return lax.dot_general(a, b, dims, preferred_element_type=F32)


def call(body, outs, scratch=(), spots=(), cost=None, kept=None, room=12):
    specs = [pl.BlockSpec(memory_space=spot) for spot in spots]
    return pl.pallas_call(
        body,
        out_shape=[jax.ShapeDtypeStruct(shape, dtype) for shape, dtype in outs],
        scratch_shapes=list(scratch),
        compiler_params=pltpu.CompilerParams(vmem_limit_bytes=room * 2**20),
        cost_estimate=cost and pl.CostEstimate(flops=cost, bytes_accessed=0, transcendentals=0),
        **({"in_specs": specs} if specs else {}),
        **({"out_specs": [pl.BlockSpec(memory_space=m) for m in kept]} if kept else {}),
    )


VM, HBM = pltpu.VMEM, pltpu.HBM
MARK = ((8, HEAD_DIM), jnp.float32)


def mark(ref):
    ref[...] = jnp.zeros_like(ref)


def halves():
    core = lax.axis_index("core")
    mine = pl.ds(pl.multiple_of(core * WIDE, WIDE), WIDE)
    other = pl.ds(pl.multiple_of((1 - core) * WIDE, WIDE), WIDE)
    return mine, other


def rows():
    core = lax.axis_index("core")
    mine = pl.ds(pl.multiple_of(core * TOK, TOK), TOK)
    other = pl.ds(pl.multiple_of((1 - core) * TOK, TOK), TOK)
    return mine, other


def head(h):
    return pl.ds(h * HEAD_DIM, HEAD_DIM)


def block(b):
    return pl.ds(b * TOK, TOK)


def quarter(i):
    return pl.ds(i * PIECE, PIECE)


def line(shift):
    core = lax.axis_index("core")
    place = lax.axis_index("x") * (1 - core) + lax.axis_index("y") * core
    return lax.rem(place + SIDE + shift, SIDE)


def cross(shift):
    core = lax.axis_index("core")
    place = lax.axis_index("y") * (1 - core) + lax.axis_index("x") * core
    return lax.rem(place + SIDE + shift, SIDE)


def chip(across, along):
    core = lax.axis_index("core")
    return across * (SIDE - core * (SIDE - 1)) + along * (1 + core * (SIDE - 1))


def causal():
    return lax.broadcasted_iota(jnp.int32, (TOK, TOK), 0) >= lax.broadcasted_iota(
        jnp.int32, (TOK, TOK), 1
    )


def pack_body(a_ref, b_ref, send_ref, *mark_refs):
    _, other = halves()
    for ref in mark_refs:
        mark(ref)
    send_ref[:, :WIDE] = a_ref[:, other].astype(F32)
    send_ref[:, WIDE:] = b_ref[:, other].astype(F32)


def unpack(ref, got, out_ref):
    mine, _ = halves()
    at, far = rows()
    out_ref[at, :] = ref[:, mine]
    out_ref[far, :] = got.astype(BF16)


def state_body(k_ref, v_ref, got_ref, _, k2_ref, v2_ref, pieces_ref):
    unpack(k_ref, got_ref[:, :WIDE], k2_ref)
    unpack(v_ref, got_ref[:, WIDE:], v2_ref)
    for h in range(HALF):
        state = dot(k2_ref[:, head(h)], v2_ref[:, head(h)], TN)
        for i in range(SIDE):
            pieces_ref[chip(i, h)] = state[i * PIECE : (i + 1) * PIECE]


def spread_body(
    q_ref, dy_ref, got_ref, k2_ref, v2_ref,
    q2_ref, dy2_ref, mark_ref, s1, s2, s3, held_ref, sems,
):
    mark(mark_ref)
    unpack(q_ref, got_ref[:, :WIDE], q2_ref)
    unpack(dy_ref, got_ref[:, WIDE:], dy2_ref)
    copies = []
    for s, send_ref in enumerate((s1, s2, s3)):
        channels = pl.ds(pl.multiple_of(line(s + 1) * HEAD_DIM, HEAD_DIM), HEAD_DIM)
        for i, ref in enumerate((k2_ref, v2_ref, q2_ref, dy2_ref)):
            held_ref[s, :, head(i)] = ref[:, channels].astype(F32)
        copies.append(pltpu.make_async_copy(held_ref.at[s], send_ref, sems.at[s]))
        copies[-1].start()
    for copy in copies:
        copy.wait()


def line_body(
    k2_ref, v2_ref, q2_ref, dy2_ref, gain_ref, got1_ref, got2_ref, got3_ref,
    q_ref, dy_ref, gain_out, intra_ref, first_ref, k_ref, v_ref,
):
    refs = (k_ref, v_ref, q_ref, dy_ref)
    place = line(0)
    channels = pl.ds(pl.multiple_of(place * HEAD_DIM, HEAD_DIM), HEAD_DIM)
    at = pl.ds(pl.multiple_of(place * PAIR, PAIR), PAIR)
    for ref, own_ref in zip(refs, (k2_ref, v2_ref, q2_ref, dy2_ref)):
        ref[at, :] = own_ref[:, channels]
    for s, got_ref in enumerate((got1_ref, got2_ref, got3_ref)):
        at = pl.ds(pl.multiple_of(line(-1 - s) * PAIR, PAIR), PAIR)
        for i, ref in enumerate(refs):
            ref[at, :] = got_ref[:, head(i)].astype(BF16)
    whole = lax.axis_index("core") * WIDE + place * HEAD_DIM
    gain = gain_ref[:, pl.ds(pl.multiple_of(whole, HEAD_DIM), HEAD_DIM)]
    gain_out[...] = jnp.broadcast_to(gain, gain_out.shape)
    mask = causal()
    for b in range(2 * SIDE):
        k, v = k_ref[block(b), :], v_ref[block(b), :]
        weights = jnp.where(mask, dot(q_ref[block(b), :], k, NT), 0.0).astype(BF16)
        intra_ref[block(b), :] = dot(weights, v, NN)
        if b % 2 == 0:
            first_ref[b // 2] = dot(k, v, TN)


def plane_body(parts_ref, _, total_ref, sums_ref):
    running = jnp.zeros(parts_ref.shape[1:], F32)
    for p in range(SIDE * SIDE):
        sums_ref[p] = running
        running = running + parts_ref[p]
    for g in range(NZ):
        total_ref[g] = running


def before_body(sums_ref, got_ref, *out_refs):
    z = lax.axis_index("z")
    base = jnp.zeros(got_ref.shape[1:], F32)
    for g in range(NZ - 1):
        base = base + jnp.where(g < z, got_ref[g], 0.0)
    for s, ref in enumerate(out_refs):
        for j in range(SIDE):
            ref[j] = sums_ref[chip(cross(s), j)] + base


def deltas(out, g):
    inverse = lax.rsqrt(jnp.mean(out * out, axis=-1, keepdims=True) + EPSILON)
    normed = out * inverse
    mean = jnp.mean(g * normed, axis=-1, keepdims=True)
    return normed, (inverse * (g - normed * mean)).astype(BF16)


def turn_body(
    q_ref, dy_ref, gain_ref, intra_ref, first_ref, w0, w1, w2, w3,
    p0, p1, p2, p3, before_ref, pairs_ref,
):
    for s, ref in enumerate((w0, w1, w2, w3)):
        at = pl.ds(pl.multiple_of(cross(-s) * PIECE, PIECE), PIECE)
        for j in range(SIDE):
            before_ref[j, at, :] = ref[j]
    gain = gain_ref[:1, :]
    for j in range(SIDE):
        before = before_ref[j]
        for b in range(2):
            at = block(2 * j + b)
            q = q_ref[at, :]
            if b:
                before = before + first_ref[j]
            out = intra_ref[at, :] + dot(q, before.astype(BF16), NN)
            _, delta = deltas(out, dy_ref[at, :].astype(F32) * gain)
            state = dot(q, delta, TN)
            pair = pair + state if b else state
        pairs_ref[j] = pair
    for s, ref in enumerate((p0, p1, p2, p3)):
        at = pl.ds(pl.multiple_of(cross(s) * PIECE, PIECE), PIECE)
        for j in range(SIDE):
            ref[j] = pairs_ref[j, at, :]


def gather_body(p0, p1, p2, p3, before_ref, total_ref, pairs_ref, b0, b1, b2, b3):
    total = jnp.zeros(p0.shape[1:], F32)
    for s, ref in enumerate((p0, p1, p2, p3)):
        for j in range(SIDE):
            pairs_ref[chip(cross(-s), j)] = ref[j]
            total = total + ref[j]
    for g in range(NZ):
        total_ref[g] = total
    for s, ref in enumerate((b0, b1, b2, b3)):
        ref[...] = before_ref[line(s)]


def later_body(pairs_ref, got_ref, out_ref):
    z = lax.axis_index("z")
    running = jnp.zeros(got_ref.shape[1:], F32)
    for g in range(1, NZ):
        running = running + jnp.where(g > z, got_ref[g], 0.0)
    for p in reversed(range(SIDE * SIDE)):
        out_ref[p] = running
        running = running + pairs_ref[p]


def query_body(
    q2_ref, k2_ref, v2_ref, dy2_ref, gain_ref, b0, b1, b2, b3,
    send_ref, own_ref, delta_ref, before_ref, all_ref,
):
    mine, _ = halves()
    own, far = rows()
    for s, ref in enumerate((b0, b1, b2, b3)):
        before_ref[line(-s)] = ref[...]
    mask = causal()
    gains = gain_ref[:, mine]
    for h in range(HALF):
        gain = gains[:, h * HEAD_DIM : (h + 1) * HEAD_DIM]
        query = pl.ds(WIDE + h * HEAD_DIM, HEAD_DIM)
        before = before_ref[h]
        for b in range(2):
            at = block(b)
            q, k, v = q2_ref[at, head(h)], k2_ref[at, head(h)], v2_ref[at, head(h)]
            before_b = before.astype(BF16)
            if b == 0:
                before = before + dot(k, v, TN)
            weights = jnp.where(mask, dot(q, k, NT), 0.0).astype(BF16)
            out = dot(weights, v, NN) + dot(q, before_b, NN)
            normed, delta = deltas(out, dy2_ref[at, head(h)].astype(F32) * gain)
            delta_ref[at, head(h)] = delta
            all_ref[at, head(h)] = normed * gain
            scores = jnp.where(mask, dot(delta, v, NT), 0.0).astype(BF16)
            all_ref[at, query] = dot(scores, k, NN) + dot(delta, before_b, NT)
    own_ref[...] = all_ref[own, :].astype(BF16)
    send_ref[...] = all_ref[far, :].astype(BF16).astype(F32)


def keys_body(q2_ref, k2_ref, v2_ref, delta_ref, gk_ref, gv_ref, second_ref):
    mask = causal()
    for h in range(HALF):
        for b in range(2):
            at = block(b)
            q, k, v = q2_ref[at, head(h)], k2_ref[at, head(h)], v2_ref[at, head(h)]
            delta = delta_ref[at, head(h)]
            weights = jnp.where(mask, dot(q, k, NT), 0.0).astype(BF16)
            scores = jnp.where(mask, dot(delta, v, NT), 0.0).astype(BF16)
            gk_ref[at, head(h)] = dot(scores, q, TN)
            gv_ref[at, head(h)] = dot(weights, delta, TN)
        second_ref[h] = dot(q, delta, TN)


def final_body(mine, k2_ref, v2_ref, later_ref, second_ref, gk_ref, gv_ref, out_ref):
    own, far = rows()
    at = own if mine else far
    core = lax.axis_index("core")
    b = core if mine else 1 - core
    for h in range(HALF):
        value = pl.ds(WIDE + h * HEAD_DIM, HEAD_DIM)
        later = jnp.concatenate([later_ref[chip(i, h)] for i in range(SIDE)], axis=0)
        after = (later + jnp.where(b == 0, second_ref[h], 0.0)).astype(BF16)
        gk = gk_ref[at, head(h)] + dot(v2_ref[at, head(h)], after, NT)
        gv = gv_ref[at, head(h)] + dot(k2_ref[at, head(h)], after, NN)
        out_ref[:, head(h)] = gk.astype(BF16).astype(out_ref.dtype)
        out_ref[:, value] = gv.astype(BF16).astype(out_ref.dtype)


def merge_body(own_ref, got_ref, a_ref, b_ref):
    mine, other = halves()
    a_ref[:, mine] = own_ref[:, :WIDE]
    a_ref[:, other] = got_ref[:, :WIDE].astype(BF16)
    b_ref[:, mine] = own_ref[:, WIDE:]
    b_ref[:, other] = got_ref[:, WIDE:].astype(BF16)


def swap(x):
    return lax.ppermute(x, "core", [(0, 1), (1, 0)])


AXES = ("z", "y", "x", "core")


def device(z, core, across, along):
    y, x = (along, across) if core else (across, along)
    return ((z * SIDE + y) * SIDE + x) * 2 + core


def places():
    return [
        (z, core, i, j) for z in range(NZ) for core in range(2) for i in range(SIDE) for j in range(SIDE)
    ]


def shift_line(arrays):
    return [
        lax.ppermute(
            a, AXES, [(device(z, c, i, j), device(z, c, i, (j + s) % SIDE)) for z, c, i, j in places()]
        )
        for s, a in enumerate(arrays, 1)
    ]


def shift_cross(arrays):
    return [
        lax.ppermute(
            a, AXES, [(device(z, c, i, j), device(z, c, (i + s) % SIDE, j)) for z, c, i, j in places()]
        )
        for s, a in enumerate(arrays, 1)
    ]


def per_device(queries, key_rows, value_rows, channel_gain, out_cotangent):
    own_shape = (TOK, HEADS * HEAD_DIM)
    pair = (PAIR, WIDE)
    slices = ((SIDE * SIDE, PIECE, HEAD_DIM), F32)
    copies = ((NZ, PIECE, HEAD_DIM), F32)
    some = ((SIDE, PIECE, HEAD_DIM), F32)
    states = ((SIDE, HEAD_DIM, HEAD_DIM), F32)
    square = ((HEAD_DIM, HEAD_DIM), F32)
    gain = channel_gain.reshape(1, -1)
    start = (1 - lax.axis_index("core")) * WIDE
    kv_send = jnp.concatenate(
        [lax.dynamic_slice_in_dim(a, start, WIDE, 1) for a in (key_rows, value_rows)], axis=1
    ).astype(F32)
    kv_got = swap(kv_send)
    qd_send, pack_done = call(pack_body, [(own_shape, F32), MARK])(queries, out_cotangent)
    qd_got = swap(qd_send)
    k2, v2, pieces = call(state_body, [(pair, BF16), (pair, BF16), slices], spots=(VM,) * 4)(
        key_rows, value_rows, kv_got, pack_done
    )
    parts = lax.all_to_all(pieces, ("y", "x"), 0, 0, tiled=True)
    q2, dy2, spread_done, *sends = call(
        spread_body,
        [(pair, BF16)] * 2 + [MARK] + [(pair, F32)] * (SIDE - 1),
        [pltpu.VMEM((SIDE - 1,) + pair, F32), pltpu.SemaphoreType.DMA((SIDE - 1,))],
        kept=(VM,) * 3 + (HBM,) * 3,
    )(queries, out_cotangent, qd_got, k2, v2)
    run = (RUN, HEAD_DIM)
    qh, dyh, gain_h, intra_h, first = call(
        line_body,
        [(run, BF16), (run, BF16), ((8, HEAD_DIM), F32), (run, F32), states],
        [pltpu.VMEM(run, BF16), pltpu.VMEM(run, BF16)],
        cost=10**11,
    )(k2, v2, q2, dy2, gain, *shift_line(sends))
    total, sums = call(plane_body, [copies, slices], spots=(VM, VM), cost=10**11)(parts, spread_done)
    earlier = lax.all_to_all(total, "z", 0, 0, tiled=True)
    w_own, *w_sends = call(before_body, [some] * SIDE)(sums, earlier)
    p_own, p1, p2, p3, before = call(
        turn_body, [some] * SIDE + [states], [pltpu.VMEM(*states)]
    )(qh, dyh, gain_h, intra_h, first, w_own, *shift_cross(w_sends))
    total, pairs, b_own, *b_sends = call(gather_body, [copies, slices] + [square] * SIDE)(
        p_own, *shift_cross((p1, p2, p3)), before
    )
    totals = lax.all_to_all(total, "z", 0, 0, tiled=True)
    b_got = shift_line(b_sends)
    (later,) = call(later_body, [slices], cost=10**11)(pairs, totals)
    send, own, delta = call(
        query_body,
        [(own_shape, F32), (own_shape, BF16), (pair, BF16)],
        [pltpu.VMEM(*states), pltpu.VMEM((PAIR, 2 * WIDE), F32)],
        cost=10**11,
    )(q2, k2, v2, dy2, gain, b_own, *b_got)
    gk, gv, second = call(keys_body, [(pair, F32), (pair, F32), states])(q2, k2, v2, delta)
    merge = call(merge_body, [(own_shape, BF16), (own_shape, BF16)])
    attended, grad_query = merge(own, swap(send))
    after = lax.all_to_all(later, ("y", "x"), 0, 0, tiled=True)
    last = (k2, v2, after, second, gk, gv)
    (last_send,) = call(functools.partial(final_body, False), [(own_shape, F32)])(*last)
    last_got = swap(last_send)
    (last_own,) = call(functools.partial(final_body, True), [(own_shape, BF16)])(*last)
    grad_key, grad_value = merge(last_own, last_got)
    return attended, grad_query, grad_key, grad_value


def solution(mesh):
    fine = Mesh(mesh.devices.reshape(NZ, SIDE, SIDE, 2), AXES)
    placed = P(AXES, None)
    return jax.shard_map(
        per_device,
        mesh=fine,
        in_specs=(placed, placed, placed, P(), placed),
        out_specs=(placed, placed, placed, placed),
        check_vma=False,
    )
```

```python
import functools

import jax
import jax.numpy as jnp
from jax import lax
from jax.experimental import pallas as pl
from jax.experimental.pallas import tpu as pltpu
from jax.sharding import Mesh, PartitionSpec as P

HEADS = 8
HEAD_DIM = 128
TOK = 128
HALF = HEADS // 2
WIDE = HALF * HEAD_DIM
PAIR = 2 * TOK
SIDE, NZ = 4, 8
RUN = SIDE * PAIR
PIECE = HEAD_DIM // SIDE
EPSILON = 1e-06
F32, BF16 = jnp.float32, jnp.bfloat16

NT = (((1,), (1,)), ((), ()))
TN = (((0,), (0,)), ((), ()))
NN = (((1,), (0,)), ((), ()))


def dot(a, b, dims):
    return lax.dot_general(a, b, dims, preferred_element_type=F32)


def call(body, outs, scratch=(), spots=(), cost=None, kept=None, room=12):
    specs = [pl.BlockSpec(memory_space=spot) for spot in spots]
    return pl.pallas_call(
        body,
        out_shape=[jax.ShapeDtypeStruct(shape, dtype) for shape, dtype in outs],
        scratch_shapes=list(scratch),
        compiler_params=pltpu.CompilerParams(vmem_limit_bytes=room * 2**20),
        cost_estimate=cost and pl.CostEstimate(flops=cost, bytes_accessed=0, transcendentals=0),
        **({"in_specs": specs} if specs else {}),
        **({"out_specs": [pl.BlockSpec(memory_space=m) for m in kept]} if kept else {}),
    )


VM, HBM = pltpu.VMEM, pltpu.HBM
MARK = ((8, HEAD_DIM), jnp.float32)


def mark(ref):
    ref[...] = jnp.zeros_like(ref)


def halves():
    core = lax.axis_index("core")
    mine = pl.ds(pl.multiple_of(core * WIDE, WIDE), WIDE)
    other = pl.ds(pl.multiple_of((1 - core) * WIDE, WIDE), WIDE)
    return mine, other


def rows():
    core = lax.axis_index("core")
    mine = pl.ds(pl.multiple_of(core * TOK, TOK), TOK)
    other = pl.ds(pl.multiple_of((1 - core) * TOK, TOK), TOK)
    return mine, other


def head(h):
    return pl.ds(h * HEAD_DIM, HEAD_DIM)


def block(b):
    return pl.ds(b * TOK, TOK)


def quarter(i):
    return pl.ds(i * PIECE, PIECE)


def line(shift):
    core = lax.axis_index("core")
    place = lax.axis_index("x") * (1 - core) + lax.axis_index("y") * core
    return lax.rem(place + SIDE + shift, SIDE)


def cross(shift):
    core = lax.axis_index("core")
    place = lax.axis_index("y") * (1 - core) + lax.axis_index("x") * core
    return lax.rem(place + SIDE + shift, SIDE)


def chip(across, along):
    core = lax.axis_index("core")
    return across * (SIDE - core * (SIDE - 1)) + along * (1 + core * (SIDE - 1))


def causal():
    return lax.broadcasted_iota(jnp.int32, (TOK, TOK), 0) >= lax.broadcasted_iota(
        jnp.int32, (TOK, TOK), 1
    )


def pack_body(a_ref, b_ref, send_ref, *mark_refs):
    _, other = halves()
    for ref in mark_refs:
        mark(ref)
    send_ref[:, :WIDE] = a_ref[:, other].astype(F32)
    send_ref[:, WIDE:] = b_ref[:, other].astype(F32)


def unpack(ref, got, out_ref):
    mine, _ = halves()
    at, far = rows()
    out_ref[at, :] = ref[:, mine]
    out_ref[far, :] = got.astype(BF16)


def state_body(k_ref, v_ref, got_ref, _, k2_ref, v2_ref, pieces_ref):
    unpack(k_ref, got_ref[:, :WIDE], k2_ref)
    unpack(v_ref, got_ref[:, WIDE:], v2_ref)
    for h in range(HALF):
        state = dot(k2_ref[:, head(h)], v2_ref[:, head(h)], TN)
        for i in range(SIDE):
            pieces_ref[chip(i, h)] = state[i * PIECE : (i + 1) * PIECE]


def spread_body(
    q_ref, dy_ref, got_ref, k2_ref, v2_ref,
    q2_ref, dy2_ref, mark_ref, s1, s2, s3, held_ref, sems,
):
    mark(mark_ref)
    unpack(q_ref, got_ref[:, :WIDE], q2_ref)
    unpack(dy_ref, got_ref[:, WIDE:], dy2_ref)
    copies = []
    for s, send_ref in enumerate((s1, s2, s3)):
        channels = pl.ds(pl.multiple_of(line(s + 1) * HEAD_DIM, HEAD_DIM), HEAD_DIM)
        for i, ref in enumerate((k2_ref, v2_ref, q2_ref, dy2_ref)):
            held_ref[s, :, head(i)] = ref[:, channels].astype(F32)
        copies.append(pltpu.make_async_copy(held_ref.at[s], send_ref, sems.at[s]))
        copies[-1].start()
    for copy in copies:
        copy.wait()


def line_body(
    k2_ref, v2_ref, q2_ref, dy2_ref, gain_ref, got1_ref, got2_ref, got3_ref,
    q_ref, dy_ref, gain_out, intra_ref, first_ref, k_ref, v_ref,
):
    refs = (k_ref, v_ref, q_ref, dy_ref)
    place = line(0)
    channels = pl.ds(pl.multiple_of(place * HEAD_DIM, HEAD_DIM), HEAD_DIM)
    at = pl.ds(pl.multiple_of(place * PAIR, PAIR), PAIR)
    for ref, own_ref in zip(refs, (k2_ref, v2_ref, q2_ref, dy2_ref)):
        ref[at, :] = own_ref[:, channels]
    for s, got_ref in enumerate((got1_ref, got2_ref, got3_ref)):
        at = pl.ds(pl.multiple_of(line(-1 - s) * PAIR, PAIR), PAIR)
        for i, ref in enumerate(refs):
            ref[at, :] = got_ref[:, head(i)].astype(BF16)
    whole = lax.axis_index("core") * WIDE + place * HEAD_DIM
    gain = gain_ref[:, pl.ds(pl.multiple_of(whole, HEAD_DIM), HEAD_DIM)]
    gain_out[...] = jnp.broadcast_to(gain, gain_out.shape)
    mask = causal()
    for b in range(2 * SIDE):
        k, v = k_ref[block(b), :], v_ref[block(b), :]
        weights = jnp.where(mask, dot(q_ref[block(b), :], k, NT), 0.0).astype(BF16)
        intra_ref[block(b), :] = dot(weights, v, NN)
        if b % 2 == 0:
            first_ref[b // 2] = dot(k, v, TN)


def plane_body(parts_ref, _, total_ref, sums_ref):
    running = jnp.zeros(parts_ref.shape[1:], F32)
    for p in range(SIDE * SIDE):
        sums_ref[p] = running
        running = running + parts_ref[p]
    for g in range(NZ):
        total_ref[g] = running


def before_body(sums_ref, got_ref, *out_refs):
    z = lax.axis_index("z")
    base = jnp.zeros(got_ref.shape[1:], F32)
    for g in range(NZ - 1):
        base = base + jnp.where(g < z, got_ref[g], 0.0)
    for s, ref in enumerate(out_refs):
        for j in range(SIDE):
            ref[j] = sums_ref[chip(cross(s), j)] + base


def deltas(out, g):
    inverse = lax.rsqrt(jnp.mean(out * out, axis=-1, keepdims=True) + EPSILON)
    normed = out * inverse
    mean = jnp.mean(g * normed, axis=-1, keepdims=True)
    return normed, (inverse * (g - normed * mean)).astype(BF16)


def turn_body(
    q_ref, dy_ref, gain_ref, intra_ref, first_ref, w0, w1, w2, w3,
    p0, p1, p2, p3, before_ref, pairs_ref,
):
    for s, ref in enumerate((w0, w1, w2, w3)):
        at = pl.ds(pl.multiple_of(cross(-s) * PIECE, PIECE), PIECE)
        for j in range(SIDE):
            before_ref[j, at, :] = ref[j]
    gain = gain_ref[:1, :]
    for j in range(SIDE):
        before = before_ref[j]
        for b in range(2):
            at = block(2 * j + b)
            q = q_ref[at, :]
            if b:
                before = before + first_ref[j]
            out = intra_ref[at, :] + dot(q, before.astype(BF16), NN)
            _, delta = deltas(out, dy_ref[at, :].astype(F32) * gain)
            state = dot(q, delta, TN)
            pair = pair + state if b else state
        pairs_ref[j] = pair
    for s, ref in enumerate((p0, p1, p2, p3)):
        at = pl.ds(pl.multiple_of(cross(s) * PIECE, PIECE), PIECE)
        for j in range(SIDE):
            ref[j] = pairs_ref[j, at, :]


def gather_body(p0, p1, p2, p3, before_ref, total_ref, pairs_ref, b0, b1, b2, b3):
    total = jnp.zeros(p0.shape[1:], F32)
    for s, ref in enumerate((p0, p1, p2, p3)):
        for j in range(SIDE):
            pairs_ref[chip(cross(-s), j)] = ref[j]
            total = total + ref[j]
    for g in range(NZ):
        total_ref[g] = total
    for s, ref in enumerate((b0, b1, b2, b3)):
        ref[...] = before_ref[line(s)]


def later_body(pairs_ref, got_ref, out_ref):
    z = lax.axis_index("z")
    running = jnp.zeros(got_ref.shape[1:], F32)
    for g in range(1, NZ):
        running = running + jnp.where(g > z, got_ref[g], 0.0)
    for p in reversed(range(SIDE * SIDE)):
        out_ref[p] = running
        running = running + pairs_ref[p]


def query_body(
    q2_ref, k2_ref, v2_ref, dy2_ref, gain_ref, b0, b1, b2, b3,
    send_ref, own_ref, delta_ref, weights_ref, scores_ref, before_ref, all_ref,
):
    mine, _ = halves()
    own, far = rows()
    for s, ref in enumerate((b0, b1, b2, b3)):
        before_ref[line(-s)] = ref[...]
    mask = causal()
    gains = gain_ref[:, mine]
    for h in range(HALF):
        gain = gains[:, h * HEAD_DIM : (h + 1) * HEAD_DIM]
        query = pl.ds(WIDE + h * HEAD_DIM, HEAD_DIM)
        before = before_ref[h]
        for b in range(2):
            at = block(b)
            q, k, v = q2_ref[at, head(h)], k2_ref[at, head(h)], v2_ref[at, head(h)]
            before_b = before.astype(BF16)
            if b == 0:
                before = before + dot(k, v, TN)
            weights = jnp.where(mask, dot(q, k, NT), 0.0).astype(BF16)
            weights_ref[h, b] = weights
            out = dot(weights, v, NN) + dot(q, before_b, NN)
            normed, delta = deltas(out, dy2_ref[at, head(h)].astype(F32) * gain)
            delta_ref[at, head(h)] = delta
            all_ref[at, head(h)] = normed * gain
            scores = jnp.where(mask, dot(delta, v, NT), 0.0).astype(BF16)
            scores_ref[h, b] = scores
            all_ref[at, query] = dot(scores, k, NN) + dot(delta, before_b, NT)
    own_ref[...] = all_ref[own, :].astype(BF16)
    send_ref[...] = all_ref[far, :].astype(BF16).astype(F32)


def keys_body(q2_ref, delta_ref, weights_ref, scores_ref, gk_ref, gv_ref, second_ref):
    for h in range(HALF):
        for b in range(2):
            at = block(b)
            q, delta = q2_ref[at, head(h)], delta_ref[at, head(h)]
            gk_ref[at, head(h)] = dot(scores_ref[h, b], q, TN)
            gv_ref[at, head(h)] = dot(weights_ref[h, b], delta, TN)
        second_ref[h] = dot(q, delta, TN)


def final_body(mine, k2_ref, v2_ref, later_ref, second_ref, gk_ref, gv_ref, out_ref):
    own, far = rows()
    at = own if mine else far
    core = lax.axis_index("core")
    b = core if mine else 1 - core
    for h in range(HALF):
        value = pl.ds(WIDE + h * HEAD_DIM, HEAD_DIM)
        later = jnp.concatenate([later_ref[chip(i, h)] for i in range(SIDE)], axis=0)
        after = (later + jnp.where(b == 0, second_ref[h], 0.0)).astype(BF16)
        gk = gk_ref[at, head(h)] + dot(v2_ref[at, head(h)], after, NT)
        gv = gv_ref[at, head(h)] + dot(k2_ref[at, head(h)], after, NN)
        out_ref[:, head(h)] = gk.astype(BF16).astype(out_ref.dtype)
        out_ref[:, value] = gv.astype(BF16).astype(out_ref.dtype)


def merge_body(own_ref, got_ref, a_ref, b_ref):
    mine, other = halves()
    a_ref[:, mine] = own_ref[:, :WIDE]
    a_ref[:, other] = got_ref[:, :WIDE].astype(BF16)
    b_ref[:, mine] = own_ref[:, WIDE:]
    b_ref[:, other] = got_ref[:, WIDE:].astype(BF16)


def swap(x):
    return lax.ppermute(x, "core", [(0, 1), (1, 0)])


AXES = ("z", "y", "x", "core")


def device(z, core, across, along):
    y, x = (along, across) if core else (across, along)
    return ((z * SIDE + y) * SIDE + x) * 2 + core


def places():
    return [
        (z, core, i, j) for z in range(NZ) for core in range(2) for i in range(SIDE) for j in range(SIDE)
    ]


def shift_line(arrays):
    return [
        lax.ppermute(
            a, AXES, [(device(z, c, i, j), device(z, c, i, (j + s) % SIDE)) for z, c, i, j in places()]
        )
        for s, a in enumerate(arrays, 1)
    ]


def shift_cross(arrays):
    return [
        lax.ppermute(
            a, AXES, [(device(z, c, i, j), device(z, c, (i + s) % SIDE, j)) for z, c, i, j in places()]
        )
        for s, a in enumerate(arrays, 1)
    ]


def per_device(queries, key_rows, value_rows, channel_gain, out_cotangent):
    own_shape = (TOK, HEADS * HEAD_DIM)
    pair = (PAIR, WIDE)
    slices = ((SIDE * SIDE, PIECE, HEAD_DIM), F32)
    copies = ((NZ, PIECE, HEAD_DIM), F32)
    some = ((SIDE, PIECE, HEAD_DIM), F32)
    states = ((SIDE, HEAD_DIM, HEAD_DIM), F32)
    square = ((HEAD_DIM, HEAD_DIM), F32)
    gain = channel_gain.reshape(1, -1)
    start = (1 - lax.axis_index("core")) * WIDE
    kv_send = jnp.concatenate(
        [lax.dynamic_slice_in_dim(a, start, WIDE, 1) for a in (key_rows, value_rows)], axis=1
    ).astype(F32)
    kv_got = swap(kv_send)
    qd_send, pack_done = call(pack_body, [(own_shape, F32), MARK])(queries, out_cotangent)
    qd_got = swap(qd_send)
    k2, v2, pieces = call(state_body, [(pair, BF16), (pair, BF16), slices], spots=(VM,) * 4)(
        key_rows, value_rows, kv_got, pack_done
    )
    parts = lax.all_to_all(pieces, ("y", "x"), 0, 0, tiled=True)
    q2, dy2, spread_done, *sends = call(
        spread_body,
        [(pair, BF16)] * 2 + [MARK] + [(pair, F32)] * (SIDE - 1),
        [pltpu.VMEM((SIDE - 1,) + pair, F32), pltpu.SemaphoreType.DMA((SIDE - 1,))],
        kept=(VM,) * 3 + (HBM,) * 3,
    )(queries, out_cotangent, qd_got, k2, v2)
    run = (RUN, HEAD_DIM)
    qh, dyh, gain_h, intra_h, first = call(
        line_body,
        [(run, BF16), (run, BF16), ((8, HEAD_DIM), F32), (run, F32), states],
        [pltpu.VMEM(run, BF16), pltpu.VMEM(run, BF16)],
        cost=10**11,
    )(k2, v2, q2, dy2, gain, *shift_line(sends))
    total, sums = call(plane_body, [copies, slices], spots=(VM, VM), cost=10**11)(parts, spread_done)
    earlier = lax.all_to_all(total, "z", 0, 0, tiled=True)
    w_own, *w_sends = call(before_body, [some] * SIDE)(sums, earlier)
    p_own, p1, p2, p3, before = call(
        turn_body, [some] * SIDE + [states], [pltpu.VMEM(*states)]
    )(qh, dyh, gain_h, intra_h, first, w_own, *shift_cross(w_sends))
    total, pairs, b_own, *b_sends = call(gather_body, [copies, slices] + [square] * SIDE)(
        p_own, *shift_cross((p1, p2, p3)), before
    )
    totals = lax.all_to_all(total, "z", 0, 0, tiled=True)
    b_got = shift_line(b_sends)
    (later,) = call(later_body, [slices], cost=10**11)(pairs, totals)
    send, own, delta, weights, scores = call(
        query_body,
        [(own_shape, F32), (own_shape, BF16), (pair, BF16)] + [((HALF, 2, TOK, TOK), BF16)] * 2,
        [pltpu.VMEM(*states), pltpu.VMEM((PAIR, 2 * WIDE), F32)],
        cost=10**11,
    )(q2, k2, v2, dy2, gain, b_own, *b_got)
    gk, gv, second = call(keys_body, [(pair, F32), (pair, F32), states])(q2, delta, weights, scores)
    merge = call(merge_body, [(own_shape, BF16), (own_shape, BF16)])
    attended, grad_query = merge(own, swap(send))
    after = lax.all_to_all(later, ("y", "x"), 0, 0, tiled=True)
    last = (k2, v2, after, second, gk, gv)
    (last_send,) = call(functools.partial(final_body, False), [(own_shape, F32)])(*last)
    last_got = swap(last_send)
    (last_own,) = call(functools.partial(final_body, True), [(own_shape, BF16)])(*last)
    grad_key, grad_value = merge(last_own, last_got)
    return attended, grad_query, grad_key, grad_value


def solution(mesh):
    fine = Mesh(mesh.devices.reshape(NZ, SIDE, SIDE, 2), AXES)
    placed = P(AXES, None)
    return jax.shard_map(
        per_device,
        mesh=fine,
        in_specs=(placed, placed, placed, P(), placed),
        out_specs=(placed, placed, placed, placed),
        check_vma=False,
    )
```
